32 devices in a mesh: expert: 4 (over y, x), zero: 8 (over z, core).
Axes of the slice: x: 2, y: 2, z: 4, core: 2. Of those that a mesh axis runs over, the one named last changes fastest.
Arguments:
- tokens: bfloat16 [4096, 1024], P(('expert', 'zero')), may hold values from -6 to 6
- grads_out: bfloat16 [4096, 1024], P(('expert', 'zero')), may hold values from -1.1953125 to 1.1953125
- routes: int32 [4096, 2], P(('expert', 'zero')), may hold values from 0 to 3, as said below
- slots: int32 [4096, 2], P(('expert', 'zero')), may hold values from 0 to 64, as said below
- combine: bfloat16 [4096, 2], P(('expert', 'zero')), may hold values from 0.049804688 to 1
- w_in: bfloat16 [4, 1024, 4096], P('expert', None, 'zero'), may hold values from -0.1875 to 0.1875
- b_in: bfloat16 [4, 4096], P('expert', 'zero'), may hold values from -3 to 3
- w_out: bfloat16 [4, 4096, 1024], P('expert', 'zero'), may hold values from -0.09375 to 0.09375
- b_out: bfloat16 [4, 1024], P('expert'), may hold values from -0.59765625 to 0.59765625
Outputs:
- grad_tokens: bfloat16 [4096, 1024], P(('expert', 'zero'))
- grad_combine: float32 [4096, 2], P(('expert', 'zero'))
- grad_w_in: bfloat16 [4, 1024, 4096], P('expert', None, 'zero')
- grad_b_in: float32 [4, 4096], P('expert', 'zero')
- grad_w_out: bfloat16 [4, 4096, 1024], P('expert', 'zero')
- grad_b_out: float32 [4, 1024], P('expert')
The draws below stay inside these ranges and needn't reach their ends.
Inputs may be any that keep to these rules, and one draw needn't show every extreme that they name: `routes`: each row names 2 different experts. Within the rows of one device (aligned blocks of 128 rows), the choices that name one expert, taken in order of row and then of column, hold the slots 0, 1, 2 and so on; once 64 of them are taken, every further such choice holds 64 and is dropped.
All inputs are finite; a program needn't handle non-finite values.
Results may differ from the reference program's by a relative error of at most 0.0065.
Values may be sent and summed in bfloat16 or wider, within the bound.
A program may use at most 128 MiB of HBM per device.

```python
import jax
import jax.numpy as jnp
from jax import lax

D = 1024
FF = 4096
TOK_DEV = 128
TOP = 2
EXPERT_COUNT = 4
CAP = 64
TOKENS = 4096
N_EXPERT = 4
N_ZERO = 8


def assignments(key):
    blocks = TOKENS // TOK_DEV
    key_hot, key_pop, key_base, key_perm = jax.random.split(key, 4)
    hot_expert = jax.random.randint(key_hot, (), 0, EXPERT_COUNT)
    popular_expert = jax.random.randint(key_pop, (EXPERT_COUNT,), 0, 4)
    baseline_score = jax.random.randint(key_base, (TOKENS, EXPERT_COUNT), 0, 4096)

    def shuffle(one_key):
        return jax.random.permutation(one_key, TOK_DEV)
    ranks = jax.vmap(shuffle)(jax.random.split(key_perm, blocks))
    forced_expert = (ranks <= CAP).reshape(TOKENS)
    expert_positions = jnp.arange(EXPERT_COUNT, dtype=jnp.int32)
    extra_score = jnp.where(forced_expert[:, None] & (expert_positions[None, :] == hot_expert), 100000, 0)
    routing_score = (baseline_score + popular_expert[None, :] * 2048 + extra_score) * EXPERT_COUNT + expert_positions[None, :]
    _, chosen = lax.top_k(routing_score, TOP)
    chosen = chosen.astype(jnp.int32)
    named = (chosen.reshape(blocks, TOK_DEV * TOP)[:, :, None] == expert_positions[None, None, :]).astype(jnp.int32)
    before = jnp.cumsum(named, axis=1) - named
    position = jnp.sum(before * named, axis=2)
    position = jnp.minimum(position, CAP).reshape(TOKENS, TOP).astype(jnp.int32)
    return (chosen, position)


def draw_routes(key, part):
    chosen, position = assignments(key)
    return chosen


def draw_slots(key, part):
    chosen, position = assignments(key)
    return position


def levels(rng, dims, shards, low, top_value):
    level, own = 1.0, jax.random.fold_in(rng, 6)
    for dim, shards_of in shards:
        heights = jnp.exp(jax.random.uniform(jax.random.fold_in(own, dim), (shards_of,), jnp.float32, low / len(shards), top_value / len(shards)))
        level = level * jnp.repeat(heights, dims[dim] // shards_of).reshape([-1 if axis == dim else 1 for axis in range(len(dims))])
    return level


def scatter_about(key, dims, deviation, bound, cuts=(), kind=jnp.bfloat16):
    values = deviation * jax.random.normal(key, dims, jnp.float32)
    if cuts:
        values = values * levels(key, dims, cuts, -0.22, 0.18)
    return jnp.clip(values, -bound, bound).astype(kind)


def setup_inputs(seed: int = 0) -> dict:
    splits = jax.random.split(jax.random.key(seed), 10)
    return {
        "tokens": scatter_about(splits[0], (TOKENS, D), 1.0, 6.0, ((0, 32),)),
        "grads_out": scatter_about(splits[1], (TOKENS, D), 0.2, 1.1953125, ((0, 32),)),
        "routes": draw_routes(jax.random.fold_in(splits[9], 71), 0),
        "slots": draw_slots(jax.random.fold_in(splits[9], 71), 0),
        "combine": jnp.clip(0.049804688 + 0.9501953 * jax.random.uniform(splits[4], (TOKENS, TOP), jnp.float32) ** levels(splits[4], (TOKENS, TOP), ((0, 32),), -0.2, 0.2), 0.049804688, 1.0).astype(jnp.bfloat16),
        "w_in": scatter_about(splits[5], (EXPERT_COUNT, D, FF), D ** -0.5, 0.1875, ((0, 4), (2, 8))),
        "b_in": scatter_about(splits[6], (EXPERT_COUNT, FF), 0.5, 3.0, ((0, 4), (1, 8))),
        "w_out": scatter_about(splits[7], (EXPERT_COUNT, FF, D), FF ** -0.5, 0.09375, ((0, 4), (1, 8))),
        "b_out": scatter_about(splits[8], (EXPERT_COUNT, D), 0.1, 0.59765625, ((0, 4),)),
    }


def gelu_parts(pre):
    cdf = 0.5 * (1.0 + lax.erf(pre * 0.7071067811865476))
    dens = jnp.exp(-0.5 * pre * pre) * 0.3989422804014327
    return pre * cdf, cdf + pre * dens


def grouped_sum(left, right):
    left_g = left.reshape(N_EXPERT, N_ZERO, CAP, -1).transpose(1, 0, 2, 3).reshape(N_ZERO, N_EXPERT * CAP, -1)
    right_g = right.reshape(N_EXPERT, N_ZERO, CAP, -1).transpose(1, 0, 2, 3).reshape(N_ZERO, N_EXPERT * CAP, -1)

    def add_group(total, pair):
        part = jnp.dot(pair[0].T, pair[1], preferred_element_type=jnp.float32).astype(jnp.bfloat16)
        part = lax.optimization_barrier(part)
        return total + part.astype(jnp.float32), None

    start = jnp.zeros((left.shape[1], right.shape[1]), jnp.float32)
    total, _ = lax.scan(add_group, start, (left_g, right_g))
    return total.astype(jnp.bfloat16)


def expert_backward(items):
    w_in, b_in, w_out, b_out, rows_x, rows_g, rows_c = items
    pre = jnp.dot(rows_x, w_in, preferred_element_type=jnp.float32) + b_in.astype(jnp.float32)[None, :]
    hidden32, slope = gelu_parts(pre)
    hidden = hidden32.astype(jnp.bfloat16)
    back = jnp.dot(rows_g, w_out.T, preferred_element_type=jnp.float32)
    weight = rows_c.astype(jnp.float32)[:, None]
    dcomb = jnp.sum(hidden32 * back, axis=1) + jnp.sum(rows_g.astype(jnp.float32) * b_out.astype(jnp.float32)[None, :], axis=1)
    dout = (weight * rows_g.astype(jnp.float32)).astype(jnp.bfloat16)
    dpre = (weight * back * slope).astype(jnp.bfloat16)
    grad_in = grouped_sum(rows_x, dpre)
    grad_bias_in = jnp.sum(dpre.astype(jnp.float32), axis=0)
    grad_out = grouped_sum(hidden, dout)
    grad_bias_out = jnp.sum(dout.astype(jnp.float32), axis=0)
    slot_dx = jnp.dot(dpre, w_in.T, preferred_element_type=jnp.float32)
    return grad_in, grad_bias_in, grad_out, grad_bias_out, slot_dx, dcomb


def reference(tokens, grads_out, routes, slots, combine, w_in, b_in, w_out, b_out):
    blocks = TOKENS // TOK_DEV
    depth = blocks * CAP
    block_of = (jnp.arange(TOKENS, dtype=jnp.int32) // TOK_DEV).astype(jnp.int32)
    kept = slots < CAP
    places = jnp.where(kept, block_of[:, None] * CAP + slots, depth).astype(jnp.int32)
    flat_e = routes.reshape(-1).astype(jnp.int32)
    flat_p = places.reshape(-1).astype(jnp.int32)
    rep_x = jnp.repeat(tokens, TOP, axis=0)
    rep_g = jnp.repeat(grads_out, TOP, axis=0)
    buf_x = jnp.zeros((EXPERT_COUNT, depth, D), tokens.dtype).at[flat_e, flat_p].set(rep_x, mode="drop")
    buf_g = jnp.zeros((EXPERT_COUNT, depth, D), grads_out.dtype).at[flat_e, flat_p].set(rep_g, mode="drop")
    buf_c = jnp.zeros((EXPERT_COUNT, depth), combine.dtype).at[flat_e, flat_p].set(combine.reshape(-1), mode="drop")
    grad_w_in, grad_b_in, grad_w_out, grad_b_out, slot_dx, slot_dc = lax.map(
        expert_backward, (w_in, b_in, w_out, b_out, buf_x, buf_g, buf_c))
    safe_p = jnp.where(kept, places, 0).astype(jnp.int32)
    keep32 = kept.astype(jnp.float32)
    picked_dx = slot_dx[routes, safe_p] * keep32[:, :, None]
    grad_tokens = jnp.sum(picked_dx, axis=1).astype(jnp.bfloat16)
    grad_combine = slot_dc[routes, safe_p] * keep32
    return grad_tokens, grad_combine, grad_w_in, grad_b_in, grad_w_out, grad_b_out
```

```python
import jax
import jax.numpy as jnp
from jax import lax
from jax.sharding import PartitionSpec as P

TOP = 2


def gelu_parts(pre):
    cdf = 0.5 * (1.0 + lax.erf(pre * 0.7071067811865476))
    dens = jnp.exp(-0.5 * pre * pre) * 0.3989422804014327
    return (pre * cdf, cdf + pre * dens)


def on_device(tokens, grads_out, routes, slots, combine, w_in, b_in, w_out, b_out):
    f32, bf16 = jnp.float32, jnp.bfloat16
    n_expert = lax.axis_size("expert")
    n_zero = lax.axis_size("zero")
    tok_rows, dim = tokens.shape
    cap_rows = TOP * tok_rows // n_expert
    width = n_expert * cap_rows
    spots = jnp.arange(width, dtype=jnp.int32)
    places = jnp.where(slots < cap_rows, routes * cap_rows + slots, -1)
    picks = (places[:, :, None] == spots[None, None, :]).astype(bf16)
    both = picks[:, 0] + picks[:, 1]
    pair = jnp.concatenate([tokens, grads_out], axis=1)
    send = jnp.einsum("tp,td->pd", both, pair, preferred_element_type=f32).astype(bf16)
    send_c = jnp.einsum("tkp,tk->p", picks, combine, preferred_element_type=f32).astype(bf16)
    send = jnp.concatenate([send, jnp.broadcast_to(send_c[:, None], (width, 128))], axis=1)
    got = lax.all_to_all(
        send.reshape(n_expert, cap_rows, -1), "expert", split_axis=0, concat_axis=0, tiled=True
    ).reshape(width, -1)
    rows = lax.all_gather(got, "zero", axis=0, tiled=True)
    rows_x = rows[:, :dim]
    rows_g = rows[:, dim : 2 * dim]
    weight = rows[:, 2 * dim : 2 * dim + 1].astype(f32)
    pre = jnp.dot(rows_x, w_in[0], preferred_element_type=f32) + b_in.astype(f32)
    hidden32, slope = gelu_parts(pre)
    back = jnp.einsum("rd,fd->rf", rows_g, w_out[0], preferred_element_type=f32)
    inner = jnp.sum(hidden32 * back, axis=1)
    hidden = hidden32.astype(bf16)
    dpre = (weight * back * slope).astype(bf16)
    dout = (weight * rows_g.astype(f32)).astype(bf16)
    slot_dx = jnp.einsum("rf,df->rd", dpre, w_in[0], preferred_element_type=f32).astype(bf16)
    part_dx = lax.all_to_all(
        slot_dx.reshape(n_zero, width, dim), "zero", split_axis=0, concat_axis=0, tiled=True
    )
    sum_dx = jnp.sum(part_dx.astype(f32), axis=0).astype(bf16)
    part_dc = lax.all_to_all(
        inner.reshape(n_zero, width), "zero", split_axis=0, concat_axis=0, tiled=True
    )
    bias_dc = jnp.sum(got[:, dim : 2 * dim].astype(f32) * b_out.astype(f32), axis=1)
    sum_dc = jnp.sum(part_dc, axis=0) + bias_dc
    grad_w_in = jnp.einsum("ra,rb->ab", rows_x, dpre, preferred_element_type=f32).astype(bf16)
    grad_w_out = jnp.einsum("ra,rb->ab", hidden, dout, preferred_element_type=f32).astype(bf16)
    grad_b_in = jnp.sum(dpre.astype(f32), axis=0)
    grad_b_out = jnp.sum(dout.astype(f32), axis=0)
    back_dx, back_dc = (
        lax.all_to_all(
            sum_dx.reshape(n_expert, cap_rows, -1), "expert", split_axis=0, concat_axis=0, tiled=True
        ),
        lax.all_to_all(
            sum_dc.reshape(n_expert, cap_rows), "expert", split_axis=0, concat_axis=0, tiled=True
        ),
    )
    grad_tokens = jnp.dot(
        both, back_dx.reshape(width, -1), preferred_element_type=f32
    ).astype(bf16)
    grad_combine = jnp.sum(picks.astype(f32) * back_dc.reshape(width), axis=2)
    return (grad_tokens, grad_combine, grad_w_in[None], grad_b_in[None], grad_w_out[None], grad_b_out[None])


def solution(mesh):
    in_specs = (
        P(("expert", "zero"), None),
        P(("expert", "zero"), None),
        P(("expert", "zero"), None),
        P(("expert", "zero"), None),
        P(("expert", "zero"), None),
        P("expert", None, "zero"),
        P("expert", "zero"),
        P("expert", "zero", None),
        P("expert", None),
    )
    out_specs = (
        P(("expert", "zero"), None),
        P(("expert", "zero"), None),
        P("expert", None, "zero"),
        P("expert", "zero"),
        P("expert", "zero", None),
        P("expert", None),
    )
    return jax.shard_map(
        on_device, mesh=mesh, in_specs=in_specs, out_specs=out_specs, check_vma=False
    )
```

```python
import functools

import jax
import jax.numpy as jnp
from jax import lax
from jax.experimental import pallas as pl
from jax.experimental.pallas import tpu as pltpu
from jax.sharding import PartitionSpec as P

TOP = 2


def gelu_parts(pre):
    cdf = 0.5 * (1.0 + lax.erf(pre * 0.7071067811865476))
    dens = jnp.exp(-0.5 * pre * pre) * 0.3989422804014327
    return (pre * cdf, cdf + pre * dens)


def plain_device(tokens, grads_out, routes, slots, combine, w_in, b_in, w_out, b_out):
    f32, bf16 = jnp.float32, jnp.bfloat16
    n_expert = lax.axis_size("expert")
    n_zero = lax.axis_size("zero")
    tok_rows, dim = tokens.shape
    cap_rows = TOP * tok_rows // n_expert
    width = n_expert * cap_rows
    spots = jnp.arange(width, dtype=jnp.int32)
    places = jnp.where(slots < cap_rows, routes * cap_rows + slots, -1)
    picks = (places[:, :, None] == spots[None, None, :]).astype(bf16)
    both = picks[:, 0] + picks[:, 1]
    pair = jnp.concatenate([tokens, grads_out], axis=1)
    send = jnp.einsum("tp,td->pd", both, pair, preferred_element_type=f32).astype(bf16)
    send_c = jnp.einsum("tkp,tk->p", picks, combine, preferred_element_type=f32).astype(bf16)
    send = jnp.concatenate([send, jnp.broadcast_to(send_c[:, None], (width, 128))], axis=1)
    got = lax.all_to_all(
        send.reshape(n_expert, cap_rows, -1), "expert", split_axis=0, concat_axis=0, tiled=True
    ).reshape(width, -1)
    rows = lax.all_gather(got, "zero", axis=0, tiled=True)
    rows_x = rows[:, :dim]
    rows_g = rows[:, dim : 2 * dim]
    weight = rows[:, 2 * dim : 2 * dim + 1].astype(f32)
    pre = jnp.dot(rows_x, w_in[0], preferred_element_type=f32) + b_in.astype(f32)
    hidden32, slope = gelu_parts(pre)
    back = jnp.einsum("rd,fd->rf", rows_g, w_out[0], preferred_element_type=f32)
    inner = jnp.sum(hidden32 * back, axis=1)
    hidden = hidden32.astype(bf16)
    dpre = (weight * back * slope).astype(bf16)
    dout = (weight * rows_g.astype(f32)).astype(bf16)
    slot_dx = jnp.einsum("rf,df->rd", dpre, w_in[0], preferred_element_type=f32).astype(bf16)
    part_dx = lax.all_to_all(
        slot_dx.reshape(n_zero, width, dim), "zero", split_axis=0, concat_axis=0, tiled=True
    )
    sum_dx = jnp.sum(part_dx.astype(f32), axis=0).astype(bf16)
    part_dc = lax.all_to_all(
        inner.reshape(n_zero, width), "zero", split_axis=0, concat_axis=0, tiled=True
    )
    bias_dc = jnp.sum(got[:, dim : 2 * dim].astype(f32) * b_out.astype(f32), axis=1)
    sum_dc = jnp.sum(part_dc, axis=0) + bias_dc
    grad_w_in = jnp.einsum("ra,rb->ab", rows_x, dpre, preferred_element_type=f32).astype(bf16)
    grad_w_out = jnp.einsum("ra,rb->ab", hidden, dout, preferred_element_type=f32).astype(bf16)
    grad_b_in = jnp.sum(dpre.astype(f32), axis=0)
    grad_b_out = jnp.sum(dout.astype(f32), axis=0)
    back_dx, back_dc = (
        lax.all_to_all(
            sum_dx.reshape(n_expert, cap_rows, -1), "expert", split_axis=0, concat_axis=0, tiled=True
        ),
        lax.all_to_all(
            sum_dc.reshape(n_expert, cap_rows), "expert", split_axis=0, concat_axis=0, tiled=True
        ),
    )
    grad_tokens = jnp.dot(
        both, back_dx.reshape(width, -1), preferred_element_type=f32
    ).astype(bf16)
    grad_combine = jnp.sum(picks.astype(f32) * back_dc.reshape(width), axis=2)
    return (grad_tokens, grad_combine, grad_w_in[None], grad_b_in[None], grad_w_out[None], grad_b_out[None])


F32, BF16 = jnp.float32, jnp.bfloat16
CORES = 2
LANES = 128


def matmul(left, right, dims):
    return lax.dot_general(left, right, (dims, ((), ())), preferred_element_type=F32)


def split_pair(value, rows):
    high = value.astype(BF16).astype(F32)
    lane = lax.broadcasted_iota(jnp.int32, (rows, LANES), 1)
    return jnp.where(lane < LANES // 2, high, value - high).astype(BF16)


def join_pair(pair):
    return jnp.sum(pair.astype(F32), axis=1, keepdims=True) * (2.0 / LANES)


def fused_kernel(
    n_expert, chips, cap, pay_ref, w_in_ref, b_in_ref, w_out_ref, b_out_ref,
    gt_ref, gc_ref, gwi_ref, gbi_ref, gwo_ref, gbo_ref,
    tok, sendbuf, rows, hid, dpre, dout, dx, dxrecv, retsend, retrecv, fsend, frecv, facc,
    tok_s, tok_r, xy_s, xy_r, sib_s, sib_r, dx_s, dx_r, ret_s, ret_r, fin_s, fin_r,
):
    me_e = lax.axis_index("expert")
    me_z = lax.axis_index("zero")
    chip, core = me_z // CORES, me_z % CORES
    width = n_expert * cap
    toks = tok.shape[1]
    dim = w_in_ref.shape[0]
    units = w_in_ref.shape[1]
    sibling = (me_e, chip * CORES + 1 - core)

    def chunk(index):
        return pl.ds(pl.multiple_of(index * cap, cap), cap)

    def expert_peer(p):
        return lax.rem(me_e + p, n_expert)

    def chip_peer(p):
        return lax.rem(chip + p, chips)

    def order(step):
        low = chip
        high = chips - 1 - chip
        least = jnp.minimum(low, high)
        half = (step + 1) // 2
        near = jnp.where(step % 2 == 1, chip + half, chip - half)
        far = jnp.where(low < high, step, chips - 1 - step)
        return jnp.where(step <= 2 * least, near, far)

    def remote(src, dst, send, recv, device):
        return pltpu.make_async_remote_copy(
            src_ref=src, dst_ref=dst, send_sem=send, recv_sem=recv, device_id=device,
            device_id_type=pl.DeviceIdType.MESH,
        )

    def tok_copy(to, frm):
        return remote(
            tok.at[frm], tok.at[frm], tok_s.at[to], tok_r.at[frm], (me_e, to * CORES + core)
        )

    def xy_copy(src, peer, frm):
        return remote(
            sendbuf.at[src, chunk(peer)], rows.at[src * CORES + core, chunk(frm)],
            xy_s.at[src, peer], xy_r.at[src, frm], (peer, me_z),
        )

    def sib_copy(src, e, lane):
        return remote(
            rows.at[src * CORES + lane, chunk(e)], rows.at[src * CORES + lane, chunk(e)],
            sib_s.at[src, e], sib_r.at[src, e], sibling,
        )

    def dx_copy(src, lane):
        return remote(
            dx.at[src * CORES + lane], dxrecv.at[src], dx_s.at[src], dx_r.at[src], sibling
        )

    def ret_copy(src, peer, frm):
        return remote(
            retsend.at[src, chunk(peer)], retrecv.at[src, chunk(frm)],
            ret_s.at[src, peer], ret_r.at[src, frm], (peer, me_z),
        )

    def fin_copy(to, frm):
        return remote(
            fsend.at[to], frecv.at[frm], fin_s.at[to], fin_r.at[frm], (me_e, to * CORES + core)
        )

    def picks_of(src):
        meta = tok[src, :, 2 * dim :].astype(F32)
        spots = lax.broadcasted_iota(jnp.int32, (toks, width), 1).astype(F32)
        quarter = LANES // 4
        first = jnp.where(meta[:, 0:1] == spots, 1.0, 0.0)
        second = jnp.where(meta[:, quarter : quarter + 1] == spots, 1.0, 0.0)
        return first, second, meta

    def stage_tokens(src):
        @pl.when(src != chip)
        def _():
            tok_copy(src, src).wait_recv()

        first, second, meta = picks_of(src)
        quarter = LANES // 4
        both = (first + second).T.astype(BF16)
        step = 512
        for col in range(0, 2 * dim, step):
            out = matmul(both, tok[src, :, col : col + step], ((1,), (0,)))
            sendbuf[src, :, col : col + step] = out.astype(BF16)
        w0 = jnp.broadcast_to(meta[:, 2 * quarter : 2 * quarter + 1], (toks, LANES)).astype(BF16)
        w1 = jnp.broadcast_to(meta[:, 3 * quarter : 3 * quarter + 1], (toks, LANES)).astype(BF16)
        out = matmul(first.T.astype(BF16), w0, ((1,), (0,))) + matmul(
            second.T.astype(BF16), w1, ((1,), (0,))
        )
        sendbuf[src, :, 2 * dim :] = out.astype(BF16)
        for p in range(1, n_expert):
            xy_copy(src, expert_peer(p), me_e).start()
        rows[src * CORES + core, chunk(me_e), :] = sendbuf[src, chunk(me_e), :]
        sib_copy(src, me_e, core).start()

    def compute(g, extra):
        weight = rows[g, :, 2 * dim : 2 * dim + 1].astype(F32)
        inner = jnp.zeros((width, 1), F32)
        tile = 256
        for col in range(0, units, tile):
            cols = slice(col, col + tile)
            pre = matmul(rows[g, :, :dim], w_in_ref[:, cols], ((1,), (0,)))
            pre = pre + b_in_ref[:, cols].astype(F32)
            back = matmul(rows[g, :, dim : 2 * dim], w_out_ref[cols, :], ((1,), (1,)))
            hidden32, slope = gelu_parts(pre)
            inner = inner + jnp.sum(hidden32 * back, axis=1, keepdims=True)
            hid[g, :, cols] = hidden32.astype(BF16)
            dpre[g, :, cols] = (weight * back * slope).astype(BF16)
        grads = rows[g, :, dim : 2 * dim].astype(F32)
        dout[g] = (weight * grads).astype(BF16)
        bias = jnp.sum(grads * b_out_ref[...].astype(F32), axis=1, keepdims=True)
        inner = inner + bias * extra
        for col in range(0, dim, 512):
            out = matmul(dpre[g], w_in_ref[col : col + 512, :], ((1,), (1,)))
            dx[g, :, col : col + 512] = out.astype(BF16)
        dx[g, :, dim:] = split_pair(inner, width)

    def stage_rows(src):
        for p in range(1, n_expert):
            peer = expert_peer(p)
            xy_copy(src, peer, peer).wait_recv()
            sib_copy(src, peer, core).start()
        compute(src * CORES + core, jnp.where(src == chip, 1.0, 0.0))

    def stage_sibling(src):
        for e in range(n_expert):
            sib_copy(src, e, 1 - core).wait_recv()
        compute(src * CORES + 1 - core, 0.0)
        dx_copy(src, 1 - core).start()

    def stage_return(src):
        dx_copy(src, core).wait_recv()
        g = src * CORES + core
        total = dx[g, :, :dim].astype(F32) + dxrecv[src, :, :dim].astype(F32)
        retsend[src, :, :dim] = total.astype(BF16)
        pair = join_pair(dx[g, :, dim:]) + join_pair(dxrecv[src, :, dim:])
        retsend[src, :, dim:] = split_pair(pair, width)
        for p in range(1, n_expert):
            ret_copy(src, expert_peer(p), me_e).start()
        retrecv[src, chunk(me_e), :] = retsend[src, chunk(me_e), :]

    def stage_combine(src):
        for p in range(1, n_expert):
            peer = expert_peer(p)
            ret_copy(src, peer, peer).wait_recv()
        first, second, _ = picks_of(src)
        both = (first + second).astype(BF16)
        grads = matmul(both, retrecv[src, :, :dim], ((1,), (0,)))
        ext = retrecv[src, :, dim:]
        one = join_pair(matmul(first.astype(BF16), ext, ((1,), (0,))))
        two = join_pair(matmul(second.astype(BF16), ext, ((1,), (0,))))

        @pl.when(src == chip)
        def _():
            facc[:, :dim] = grads
            facc[:, dim : dim + LANES] = jnp.broadcast_to(one, (toks, LANES))
            facc[:, dim + LANES :] = jnp.broadcast_to(two, (toks, LANES))

        @pl.when(src != chip)
        def _():
            fsend[src, :, :dim] = grads.astype(BF16)
            fsend[src, :, dim : dim + LANES] = split_pair(one, toks)
            fsend[src, :, dim + LANES :] = split_pair(two, toks)
            fin_copy(src, chip).start()

    barrier = pltpu.get_barrier_semaphore()

    def greet(device):
        pl.semaphore_signal(
            barrier, inc=1, device_id=device, device_id_type=pl.DeviceIdType.MESH
        )

    for p in range(1, n_expert):
        greet((expert_peer(p), me_z))
    for p in range(1, chips):
        greet((me_e, chip_peer(p) * CORES + core))
    greet(sibling)
    tok[chip] = pay_ref[...]
    pl.semaphore_wait(barrier, n_expert + chips - 1)

    for p in range(1, chips):
        tok_copy(chip_peer(p), chip).start()

    @pl.loop(0, chips + 2)
    def _(step):
        @pl.when(step < chips)
        def _():
            stage_tokens(order(step))

        @pl.when((step >= 1) & (step < chips + 1))
        def _():
            stage_rows(order(step - 1))

        @pl.when(step >= 2)
        def _():
            stage_sibling(order(step - 2))

        @pl.when(step >= 3)
        def _():
            stage_return(order(step - 3))

        @pl.when(step >= 4)
        def _():
            stage_combine(order(step - 4))

    stage_return(order(chips - 1))
    groups = chips * CORES
    all_rows = groups * width
    d_all = dpre[...].reshape(all_rows, units)
    for col in range(0, dim, 256):
        x_all = rows[:, :, col : col + 256].reshape(all_rows, 256)
        gwi_ref[col : col + 256, :] = matmul(x_all, d_all, ((0,), (0,))).astype(BF16)
    stage_combine(order(chips - 2))
    stage_combine(order(chips - 1))
    o_all = dout[...].reshape(all_rows, dim)
    for col in range(0, units, 256):
        h_all = hid[:, :, col : col + 256].reshape(all_rows, 256)
        gwo_ref[col : col + 256, :] = matmul(h_all, o_all, ((0,), (0,))).astype(BF16)
    ones = jnp.ones((8, all_rows), BF16)
    gbi_ref[...] = matmul(ones, d_all, ((1,), (0,)))[0:1]
    gbo_ref[...] = matmul(ones, o_all, ((1,), (0,)))[0:1]

    total = facc[:, :dim]
    one = facc[:, dim : dim + 1]
    two = facc[:, dim + LANES : dim + LANES + 1]
    for p in range(1, chips):
        other = chip_peer(p)
        fin_copy(other, other).wait_recv()
        total = total + frecv[other, :, :dim].astype(F32)
        one = one + join_pair(frecv[other, :, dim : dim + LANES])
        two = two + join_pair(frecv[other, :, dim + LANES :])
    gt_ref[...] = total.astype(BF16)
    gc_ref[:, 0:1] = one
    gc_ref[:, 1:2] = two

    for p in range(1, chips):
        other = chip_peer(p)
        tok_copy(other, chip).wait_send()
        fin_copy(other, chip).wait_send()
    for src in range(chips):
        for p in range(1, n_expert):
            xy_copy(src, expert_peer(p), me_e).wait_send()
            ret_copy(src, expert_peer(p), me_e).wait_send()
        for e in range(n_expert):
            sib_copy(src, e, core).wait_send()
        dx_copy(src, 1 - core).wait_send()


def scratch_sizes(n_expert, chips, cap, toks, dim, units):
    width, groups = n_expert * cap, chips * CORES
    return [
        ((chips, toks, 2 * dim + LANES), BF16),
        ((chips, width, 2 * dim + LANES), BF16),
        ((groups, width, 2 * dim + LANES), BF16),
        ((groups, width, units), BF16),
        ((groups, width, units), BF16),
        ((groups, width, dim), BF16),
        ((groups, width, dim + LANES), BF16),
        ((chips, width, dim + LANES), BF16),
        ((chips, width, dim + LANES), BF16),
        ((chips, width, dim + LANES), BF16),
        ((chips, toks, dim + 2 * LANES), BF16),
        ((chips, toks, dim + 2 * LANES), BF16),
        ((toks, dim + 2 * LANES), F32),
    ]


def on_device(tokens, grads_out, routes, slots, combine, w_in, b_in, w_out, b_out):
    n_expert = lax.axis_size("expert")
    n_zero = lax.axis_size("zero")
    toks, dim = tokens.shape
    units = w_in.shape[2]
    cap = TOP * toks // n_expert
    chips = n_zero // CORES
    sizes = scratch_sizes(n_expert, chips, cap, toks, dim, units)
    held = sum(functools.reduce(lambda a, b: a * b, s) * jnp.dtype(t).itemsize for s, t in sizes)
    if held > (46 << 20) or n_expert * cap > 256 or n_zero % CORES or chips < 3:
        return plain_device(
            tokens, grads_out, routes, slots, combine, w_in, b_in, w_out, b_out
        )
    places = jnp.where(slots < cap, routes * cap + slots, -1).astype(BF16)
    meta = jnp.repeat(jnp.concatenate([places, combine], axis=1), LANES // 4, axis=1)
    payload = jnp.concatenate([tokens, grads_out, meta], axis=1)
    vmem = pl.BlockSpec(memory_space=pltpu.VMEM)
    sem = pltpu.SemaphoreType.DMA
    outs = pl.pallas_call(
        functools.partial(fused_kernel, n_expert, chips, cap),
        out_shape=(
            jax.ShapeDtypeStruct((toks, dim), BF16),
            jax.ShapeDtypeStruct((toks, TOP), F32),
            jax.ShapeDtypeStruct((dim, units), BF16),
            jax.ShapeDtypeStruct((1, units), F32),
            jax.ShapeDtypeStruct((units, dim), BF16),
            jax.ShapeDtypeStruct((1, dim), F32),
        ),
        in_specs=[vmem] * 5,
        out_specs=(vmem,) * 6,
        scratch_shapes=[pltpu.VMEM(s, t) for s, t in sizes]
        + [
            sem((chips,)), sem((chips,)),
            sem((chips, n_expert)), sem((chips, n_expert)),
            sem((chips, n_expert)), sem((chips, n_expert)),
            sem((chips,)), sem((chips,)),
            sem((chips, n_expert)), sem((chips, n_expert)),
            sem((chips,)), sem((chips,)),
        ],
        compiler_params=pltpu.CompilerParams(
            collective_id=0, has_side_effects=True, vmem_limit_bytes=60 << 20
        ),
        name="routed_expert_backward",
    )(payload, w_in[0], b_in, w_out[0], b_out)
    gt, gc, gwi, gbi, gwo, gbo = outs
    return (gt, gc, gwi[None], gbi, gwo[None], gbo)


def solution(mesh):
    in_specs = (
        P(("expert", "zero"), None),
        P(("expert", "zero"), None),
        P(("expert", "zero"), None),
        P(("expert", "zero"), None),
        P(("expert", "zero"), None),
        P("expert", None, "zero"),
        P("expert", "zero"),
        P("expert", "zero", None),
        P("expert", None),
    )
    out_specs = (
        P(("expert", "zero"), None),
        P(("expert", "zero"), None),
        P("expert", None, "zero"),
        P("expert", "zero"),
        P("expert", "zero", None),
        P("expert", None),
    )
    return jax.shard_map(
        on_device, mesh=mesh, in_specs=in_specs, out_specs=out_specs, check_vma=False
    )
```

```python
import functools

import jax
import jax.numpy as jnp
from jax import lax
from jax.experimental import pallas as pl
from jax.experimental.pallas import tpu as pltpu
from jax.sharding import PartitionSpec as P

TOP = 2


def gelu_parts(pre):
    cdf = 0.5 * (1.0 + lax.erf(pre * 0.7071067811865476))
    dens = jnp.exp(-0.5 * pre * pre) * 0.3989422804014327
    return (pre * cdf, cdf + pre * dens)


def plain_device(tokens, grads_out, routes, slots, combine, w_in, b_in, w_out, b_out):
    f32, bf16 = jnp.float32, jnp.bfloat16
    n_expert = lax.axis_size("expert")
    n_zero = lax.axis_size("zero")
    tok_rows, dim = tokens.shape
    cap_rows = TOP * tok_rows // n_expert
    width = n_expert * cap_rows
    spots = jnp.arange(width, dtype=jnp.int32)
    places = jnp.where(slots < cap_rows, routes * cap_rows + slots, -1)
    picks = (places[:, :, None] == spots[None, None, :]).astype(bf16)
    both = picks[:, 0] + picks[:, 1]
    pair = jnp.concatenate([tokens, grads_out], axis=1)
    send = jnp.einsum("tp,td->pd", both, pair, preferred_element_type=f32).astype(bf16)
    send_c = jnp.einsum("tkp,tk->p", picks, combine, preferred_element_type=f32).astype(bf16)
    send = jnp.concatenate([send, jnp.broadcast_to(send_c[:, None], (width, 128))], axis=1)
    got = lax.all_to_all(
        send.reshape(n_expert, cap_rows, -1), "expert", split_axis=0, concat_axis=0, tiled=True
    ).reshape(width, -1)
    rows = lax.all_gather(got, "zero", axis=0, tiled=True)
    rows_x = rows[:, :dim]
    rows_g = rows[:, dim : 2 * dim]
    weight = rows[:, 2 * dim : 2 * dim + 1].astype(f32)
    pre = jnp.dot(rows_x, w_in[0], preferred_element_type=f32) + b_in.astype(f32)
    hidden32, slope = gelu_parts(pre)
    back = jnp.einsum("rd,fd->rf", rows_g, w_out[0], preferred_element_type=f32)
    inner = jnp.sum(hidden32 * back, axis=1)
    hidden = hidden32.astype(bf16)
    dpre = (weight * back * slope).astype(bf16)
    dout = (weight * rows_g.astype(f32)).astype(bf16)
    slot_dx = jnp.einsum("rf,df->rd", dpre, w_in[0], preferred_element_type=f32).astype(bf16)
    part_dx = lax.all_to_all(
        slot_dx.reshape(n_zero, width, dim), "zero", split_axis=0, concat_axis=0, tiled=True
    )
    sum_dx = jnp.sum(part_dx.astype(f32), axis=0).astype(bf16)
    part_dc = lax.all_to_all(
        inner.reshape(n_zero, width), "zero", split_axis=0, concat_axis=0, tiled=True
    )
    bias_dc = jnp.sum(got[:, dim : 2 * dim].astype(f32) * b_out.astype(f32), axis=1)
    sum_dc = jnp.sum(part_dc, axis=0) + bias_dc
    grad_w_in = jnp.einsum("ra,rb->ab", rows_x, dpre, preferred_element_type=f32).astype(bf16)
    grad_w_out = jnp.einsum("ra,rb->ab", hidden, dout, preferred_element_type=f32).astype(bf16)
    grad_b_in = jnp.sum(dpre.astype(f32), axis=0)
    grad_b_out = jnp.sum(dout.astype(f32), axis=0)
    back_dx, back_dc = (
        lax.all_to_all(
            sum_dx.reshape(n_expert, cap_rows, -1), "expert", split_axis=0, concat_axis=0, tiled=True
        ),
        lax.all_to_all(
            sum_dc.reshape(n_expert, cap_rows), "expert", split_axis=0, concat_axis=0, tiled=True
        ),
    )
    grad_tokens = jnp.dot(
        both, back_dx.reshape(width, -1), preferred_element_type=f32
    ).astype(bf16)
    grad_combine = jnp.sum(picks.astype(f32) * back_dc.reshape(width), axis=2)
    return (grad_tokens, grad_combine, grad_w_in[None], grad_b_in[None], grad_w_out[None], grad_b_out[None])


F32, BF16 = jnp.float32, jnp.bfloat16
CORES = 2
LANES = 128


def matmul(left, right, dims):
    return lax.dot_general(left, right, (dims, ((), ())), preferred_element_type=F32)


def split_pair(value, rows):
    high = value.astype(BF16).astype(F32)
    lane = lax.broadcasted_iota(jnp.int32, (rows, LANES), 1)
    return jnp.where(lane < LANES // 2, high, value - high).astype(BF16)


def join_pair(pair):
    return jnp.sum(pair.astype(F32), axis=1, keepdims=True) * (2.0 / LANES)


def fused_kernel(
    n_expert, chips, cap, x_ref, g_ref, meta_ref, w_in_ref, b_in_ref, w_out_ref, b_out_ref,
    gt_ref, gc_ref, gwi_ref, gbi_ref, gwo_ref, gbo_ref,
    tok, sendbuf, rows, hid, dpre, dout, dx, dxrecv, retsend, retrecv, fsend, frecv, facc,
    tok_s, tok_r, xy_s, xy_r, sib_s, sib_r, dx_s, dx_r, ret_s, ret_r, fin_s, fin_r,
):
    me_e = lax.axis_index("expert")
    me_z = lax.axis_index("zero")
    chip, core = me_z // CORES, me_z % CORES
    width = n_expert * cap
    toks = tok.shape[1]
    dim = w_in_ref.shape[0]
    units = w_in_ref.shape[1]
    sibling = (me_e, chip * CORES + 1 - core)

    def chunk(index):
        return pl.ds(pl.multiple_of(index * cap, cap), cap)

    def expert_peer(p):
        return lax.rem(me_e + p, n_expert)

    def chip_peer(p):
        return lax.rem(chip + p, chips)

    def order(step):
        low = chip
        high = chips - 1 - chip
        least = jnp.minimum(low, high)
        half = (step + 1) // 2
        near = jnp.where(step % 2 == 1, chip + half, chip - half)
        far = jnp.where(low < high, step, chips - 1 - step)
        return jnp.where(step <= 2 * least, near, far)

    def remote(src, dst, send, recv, device):
        return pltpu.make_async_remote_copy(
            src_ref=src, dst_ref=dst, send_sem=send, recv_sem=recv, device_id=device,
            device_id_type=pl.DeviceIdType.MESH,
        )

    def tok_copy(src, way):
        to = chip + (1 if way else -1)
        return remote(
            tok.at[src], tok.at[src], tok_s.at[way, src], tok_r.at[src],
            (me_e, to * CORES + core),
        )

    def pass_tokens(away):
        @pl.when(chip >= away)
        def _():
            tok_copy(chip - away, 1).wait_recv()

            @pl.when(chip < chips - 1)
            def _():
                tok_copy(chip - away, 1).start()

        @pl.when(chip + away < chips)
        def _():
            tok_copy(chip + away, 0).wait_recv()

            @pl.when(chip > 0)
            def _():
                tok_copy(chip + away, 0).start()

    def xy_copy(src, peer, frm):
        return remote(
            sendbuf.at[src, chunk(peer)], rows.at[src * CORES + core, chunk(frm)],
            xy_s.at[src, peer], xy_r.at[src, frm], (peer, me_z),
        )

    def sib_copy(src, e, lane):
        return remote(
            rows.at[src * CORES + lane, chunk(e)], rows.at[src * CORES + lane, chunk(e)],
            sib_s.at[src, e], sib_r.at[src, e], sibling,
        )

    def dx_copy(src, lane):
        return remote(
            dx.at[src * CORES + lane], dxrecv.at[src], dx_s.at[src], dx_r.at[src], sibling
        )

    def ret_copy(src, peer, frm):
        return remote(
            retsend.at[src, chunk(peer)], retrecv.at[src, chunk(frm)],
            ret_s.at[src, peer], ret_r.at[src, frm], (peer, me_z),
        )

    def fin_copy(to, frm):
        return remote(
            fsend.at[to], frecv.at[frm], fin_s.at[to], fin_r.at[frm], (me_e, to * CORES + core)
        )

    def picks_of(src):
        meta = tok[src, :, 2 * dim :].astype(F32)
        spots = lax.broadcasted_iota(jnp.int32, (toks, width), 1).astype(F32)
        quarter = LANES // 4
        first = jnp.where(meta[:, 0:1] == spots, 1.0, 0.0)
        second = jnp.where(meta[:, quarter : quarter + 1] == spots, 1.0, 0.0)
        return first, second, meta

    def stage_tokens(src):
        first, second, meta = picks_of(src)
        quarter = LANES // 4
        both = (first + second).T.astype(BF16)
        step = 512
        for col in range(0, 2 * dim, step):
            out = matmul(both, tok[src, :, col : col + step], ((1,), (0,)))
            sendbuf[src, :, col : col + step] = out.astype(BF16)
        w0 = jnp.broadcast_to(meta[:, 2 * quarter : 2 * quarter + 1], (toks, LANES)).astype(BF16)
        w1 = jnp.broadcast_to(meta[:, 3 * quarter : 3 * quarter + 1], (toks, LANES)).astype(BF16)
        out = matmul(first.T.astype(BF16), w0, ((1,), (0,))) + matmul(
            second.T.astype(BF16), w1, ((1,), (0,))
        )
        sendbuf[src, :, 2 * dim :] = out.astype(BF16)
        for p in range(1, n_expert):
            xy_copy(src, expert_peer(p), me_e).start()
        rows[src * CORES + core, chunk(me_e), :] = sendbuf[src, chunk(me_e), :]
        sib_copy(src, me_e, core).start()

    def compute(g, extra):
        weight = rows[g, :, 2 * dim : 2 * dim + 1].astype(F32)
        inner = jnp.zeros((width, 1), F32)
        tile = 256
        for col in range(0, units, tile):
            cols = slice(col, col + tile)
            pre = matmul(rows[g, :, :dim], w_in_ref[:, cols], ((1,), (0,)))
            pre = pre + b_in_ref[:, cols].astype(F32)
            back = matmul(rows[g, :, dim : 2 * dim], w_out_ref[cols, :], ((1,), (1,)))
            hidden32, slope = gelu_parts(pre)
            inner = inner + jnp.sum(hidden32 * back, axis=1, keepdims=True)
            hid[g, :, cols] = hidden32.astype(BF16)
            dpre[g, :, cols] = (weight * back * slope).astype(BF16)
        grads = rows[g, :, dim : 2 * dim].astype(F32)
        dout[g] = (weight * grads).astype(BF16)
        bias = jnp.sum(grads * b_out_ref[...].astype(F32), axis=1, keepdims=True)
        inner = inner + bias * extra
        for col in range(0, dim, 512):
            out = matmul(dpre[g], w_in_ref[col : col + 512, :], ((1,), (1,)))
            dx[g, :, col : col + 512] = out.astype(BF16)
        dx[g, :, dim:] = split_pair(inner, width)

    def stage_rows(src):
        for p in range(1, n_expert):
            peer = expert_peer(p)
            xy_copy(src, peer, peer).wait_recv()
            sib_copy(src, peer, core).start()
        compute(src * CORES + core, jnp.where(src == chip, 1.0, 0.0))

    def stage_sibling(src):
        for e in range(n_expert):
            sib_copy(src, e, 1 - core).wait_recv()
        compute(src * CORES + 1 - core, 0.0)
        dx_copy(src, 1 - core).start()

    def stage_return(src):
        dx_copy(src, core).wait_recv()
        g = src * CORES + core
        total = dx[g, :, :dim].astype(F32) + dxrecv[src, :, :dim].astype(F32)
        retsend[src, :, :dim] = total.astype(BF16)
        pair = join_pair(dx[g, :, dim:]) + join_pair(dxrecv[src, :, dim:])
        retsend[src, :, dim:] = split_pair(pair, width)
        for p in range(1, n_expert):
            ret_copy(src, expert_peer(p), me_e).start()
        retrecv[src, chunk(me_e), :] = retsend[src, chunk(me_e), :]

    def stage_combine(src):
        for p in range(1, n_expert):
            peer = expert_peer(p)
            ret_copy(src, peer, peer).wait_recv()
        first, second, _ = picks_of(src)
        both = (first + second).astype(BF16)
        grads = matmul(both, retrecv[src, :, :dim], ((1,), (0,)))
        ext = retrecv[src, :, dim:]
        one = join_pair(matmul(first.astype(BF16), ext, ((1,), (0,))))
        two = join_pair(matmul(second.astype(BF16), ext, ((1,), (0,))))

        @pl.when(src == chip)
        def _():
            facc[:, :dim] = grads
            facc[:, dim : dim + LANES] = jnp.broadcast_to(one, (toks, LANES))
            facc[:, dim + LANES :] = jnp.broadcast_to(two, (toks, LANES))

        @pl.when(src != chip)
        def _():
            fsend[src, :, :dim] = grads.astype(BF16)
            fsend[src, :, dim : dim + LANES] = split_pair(one, toks)
            fsend[src, :, dim + LANES :] = split_pair(two, toks)
            fin_copy(src, chip).start()

    barrier = pltpu.get_barrier_semaphore()

    def greet(device):
        pl.semaphore_signal(
            barrier, inc=1, device_id=device, device_id_type=pl.DeviceIdType.MESH
        )

    for p in range(1, n_expert):
        greet((expert_peer(p), me_z))
    for p in range(1, chips):
        greet((me_e, chip_peer(p) * CORES + core))
    greet(sibling)
    tok[chip, :, :dim] = x_ref[...]
    tok[chip, :, dim : 2 * dim] = g_ref[...]
    tok[chip, :, 2 * dim :] = meta_ref[...]
    pl.semaphore_wait(barrier, n_expert + chips - 1)

    @pl.when(chip < chips - 1)
    def _():
        tok_copy(chip, 1).start()

    @pl.when(chip > 0)
    def _():
        tok_copy(chip, 0).start()

    @pl.loop(0, chips + 1)
    def _(step):
        @pl.when((step >= 1) & (step < chips))
        def _():
            pass_tokens(step)

        @pl.when(step < chips)
        def _():
            stage_tokens(order(step))

        @pl.when(step >= 1)
        def _():
            stage_rows(order(step - 1))
            stage_sibling(order(step - 1))

        @pl.when(step >= 2)
        def _():
            stage_combine(order(step - 2))

        @pl.when(step >= 1)
        def _():
            stage_return(order(step - 1))

    groups = chips * CORES
    all_rows = groups * width
    d_all = dpre[...].reshape(all_rows, units)
    for col in range(0, dim, 256):
        x_all = rows[:, :, col : col + 256].reshape(all_rows, 256)
        gwi_ref[col : col + 256, :] = matmul(x_all, d_all, ((0,), (0,))).astype(BF16)
    stage_combine(order(chips - 1))
    o_all = dout[...].reshape(all_rows, dim)
    for col in range(0, units, 256):
        h_all = hid[:, :, col : col + 256].reshape(all_rows, 256)
        gwo_ref[col : col + 256, :] = matmul(h_all, o_all, ((0,), (0,))).astype(BF16)
    ones = jnp.ones((8, all_rows), BF16)
    gbi_ref[...] = matmul(ones, d_all, ((1,), (0,)))[0:1]
    gbo_ref[...] = matmul(ones, o_all, ((1,), (0,)))[0:1]

    total = facc[:, :dim]
    one = facc[:, dim : dim + 1]
    two = facc[:, dim + LANES : dim + LANES + 1]
    for p in range(1, chips):
        other = chip_peer(p)
        fin_copy(other, other).wait_recv()
        total = total + frecv[other, :, :dim].astype(F32)
        one = one + join_pair(frecv[other, :, dim : dim + LANES])
        two = two + join_pair(frecv[other, :, dim + LANES :])
    gt_ref[...] = total.astype(BF16)
    gc_ref[:, 0:1] = one
    gc_ref[:, 1:2] = two

    for p in range(1, chips):
        other = chip_peer(p)
        fin_copy(other, chip).wait_send()
    for src in range(chips):
        @pl.when((src <= chip) & (chip < chips - 1))
        def _():
            tok_copy(src, 1).wait_send()

        @pl.when((src >= chip) & (chip > 0))
        def _():
            tok_copy(src, 0).wait_send()

        for p in range(1, n_expert):
            xy_copy(src, expert_peer(p), me_e).wait_send()
            ret_copy(src, expert_peer(p), me_e).wait_send()
        for e in range(n_expert):
            sib_copy(src, e, core).wait_send()
        dx_copy(src, 1 - core).wait_send()


def scratch_sizes(n_expert, chips, cap, toks, dim, units):
    width, groups = n_expert * cap, chips * CORES
    return [
        ((chips, toks, 2 * dim + LANES), BF16),
        ((chips, width, 2 * dim + LANES), BF16),
        ((groups, width, 2 * dim + LANES), BF16),
        ((groups, width, units), BF16),
        ((groups, width, units), BF16),
        ((groups, width, dim), BF16),
        ((groups, width, dim + LANES), BF16),
        ((chips, width, dim + LANES), BF16),
        ((chips, width, dim + LANES), BF16),
        ((chips, width, dim + LANES), BF16),
        ((chips, toks, dim + 2 * LANES), BF16),
        ((chips, toks, dim + 2 * LANES), BF16),
        ((toks, dim + 2 * LANES), F32),
    ]


def on_device(tokens, grads_out, routes, slots, combine, w_in, b_in, w_out, b_out):
    n_expert = lax.axis_size("expert")
    n_zero = lax.axis_size("zero")
    toks, dim = tokens.shape
    units = w_in.shape[2]
    cap = TOP * toks // n_expert
    chips = n_zero // CORES
    sizes = scratch_sizes(n_expert, chips, cap, toks, dim, units)
    held = sum(functools.reduce(lambda a, b: a * b, s) * jnp.dtype(t).itemsize for s, t in sizes)
    if held > (46 << 20) or n_expert * cap > 256 or n_zero % CORES or chips < 3:
        return plain_device(
            tokens, grads_out, routes, slots, combine, w_in, b_in, w_out, b_out
        )
    places = jnp.where(slots < cap, routes * cap + slots, -1).astype(BF16)
    meta = jnp.repeat(jnp.concatenate([places, combine], axis=1), LANES // 4, axis=1)
    vmem = pl.BlockSpec(memory_space=pltpu.VMEM)
    sem = pltpu.SemaphoreType.DMA
    outs = pl.pallas_call(
        functools.partial(fused_kernel, n_expert, chips, cap),
        out_shape=(
            jax.ShapeDtypeStruct((toks, dim), BF16),
            jax.ShapeDtypeStruct((toks, TOP), F32),
            jax.ShapeDtypeStruct((dim, units), BF16),
            jax.ShapeDtypeStruct((1, units), F32),
            jax.ShapeDtypeStruct((units, dim), BF16),
            jax.ShapeDtypeStruct((1, dim), F32),
        ),
        in_specs=[vmem] * 7,
        out_specs=(vmem,) * 6,
        scratch_shapes=[pltpu.VMEM(s, t) for s, t in sizes]
        + [
            sem((2, chips)), sem((chips,)),
            sem((chips, n_expert)), sem((chips, n_expert)),
            sem((chips, n_expert)), sem((chips, n_expert)),
            sem((chips,)), sem((chips,)),
            sem((chips, n_expert)), sem((chips, n_expert)),
            sem((chips,)), sem((chips,)),
        ],
        compiler_params=pltpu.CompilerParams(
            collective_id=0, has_side_effects=True, vmem_limit_bytes=60 << 20
        ),
        name="routed_expert_backward",
    )(tokens, grads_out, meta, w_in[0], b_in, w_out[0], b_out)
    gt, gc, gwi, gbi, gwo, gbo = outs
    return (gt, gc, gwi[None], gbi, gwo[None], gbo)


def solution(mesh):
    in_specs = (
        P(("expert", "zero"), None),
        P(("expert", "zero"), None),
        P(("expert", "zero"), None),
        P(("expert", "zero"), None),
        P(("expert", "zero"), None),
        P("expert", None, "zero"),
        P("expert", "zero"),
        P("expert", "zero", None),
        P("expert", None),
    )
    out_specs = (
        P(("expert", "zero"), None),
        P(("expert", "zero"), None),
        P("expert", None, "zero"),
        P("expert", "zero"),
        P("expert", "zero", None),
        P("expert", None),
    )
    return jax.shard_map(
        on_device, mesh=mesh, in_specs=in_specs, out_specs=out_specs, check_vma=False
    )
```

```python
import functools

import jax
import jax.numpy as jnp
from jax import lax
from jax.experimental import pallas as pl
from jax.experimental.pallas import tpu as pltpu
from jax.sharding import PartitionSpec as P

TOP = 2


def gelu_parts(pre):
    cdf = 0.5 * (1.0 + lax.erf(pre * 0.7071067811865476))
    dens = jnp.exp(-0.5 * pre * pre) * 0.3989422804014327
    return (pre * cdf, cdf + pre * dens)


def plain_device(tokens, grads_out, routes, slots, combine, w_in, b_in, w_out, b_out):
    f32, bf16 = jnp.float32, jnp.bfloat16
    n_expert = lax.axis_size("expert")
    n_zero = lax.axis_size("zero")
    tok_rows, dim = tokens.shape
    cap_rows = TOP * tok_rows // n_expert
    width = n_expert * cap_rows
    spots = jnp.arange(width, dtype=jnp.int32)
    places = jnp.where(slots < cap_rows, routes * cap_rows + slots, -1)
    picks = (places[:, :, None] == spots[None, None, :]).astype(bf16)
    both = picks[:, 0] + picks[:, 1]
    pair = jnp.concatenate([tokens, grads_out], axis=1)
    send = jnp.einsum("tp,td->pd", both, pair, preferred_element_type=f32).astype(bf16)
    send_c = jnp.einsum("tkp,tk->p", picks, combine, preferred_element_type=f32).astype(bf16)
    send = jnp.concatenate([send, jnp.broadcast_to(send_c[:, None], (width, 128))], axis=1)
    got = lax.all_to_all(
        send.reshape(n_expert, cap_rows, -1), "expert", split_axis=0, concat_axis=0, tiled=True
    ).reshape(width, -1)
    rows = lax.all_gather(got, "zero", axis=0, tiled=True)
    rows_x = rows[:, :dim]
    rows_g = rows[:, dim : 2 * dim]
    weight = rows[:, 2 * dim : 2 * dim + 1].astype(f32)
    pre = jnp.dot(rows_x, w_in[0], preferred_element_type=f32) + b_in.astype(f32)
    hidden32, slope = gelu_parts(pre)
    back = jnp.einsum("rd,fd->rf", rows_g, w_out[0], preferred_element_type=f32)
    inner = jnp.sum(hidden32 * back, axis=1)
    hidden = hidden32.astype(bf16)
    dpre = (weight * back * slope).astype(bf16)
    dout = (weight * rows_g.astype(f32)).astype(bf16)
    slot_dx = jnp.einsum("rf,df->rd", dpre, w_in[0], preferred_element_type=f32).astype(bf16)
    part_dx = lax.all_to_all(
        slot_dx.reshape(n_zero, width, dim), "zero", split_axis=0, concat_axis=0, tiled=True
    )
    sum_dx = jnp.sum(part_dx.astype(f32), axis=0).astype(bf16)
    part_dc = lax.all_to_all(
        inner.reshape(n_zero, width), "zero", split_axis=0, concat_axis=0, tiled=True
    )
    bias_dc = jnp.sum(got[:, dim : 2 * dim].astype(f32) * b_out.astype(f32), axis=1)
    sum_dc = jnp.sum(part_dc, axis=0) + bias_dc
    grad_w_in = jnp.einsum("ra,rb->ab", rows_x, dpre, preferred_element_type=f32).astype(bf16)
    grad_w_out = jnp.einsum("ra,rb->ab", hidden, dout, preferred_element_type=f32).astype(bf16)
    grad_b_in = jnp.sum(dpre.astype(f32), axis=0)
    grad_b_out = jnp.sum(dout.astype(f32), axis=0)
    back_dx, back_dc = (
        lax.all_to_all(
            sum_dx.reshape(n_expert, cap_rows, -1), "expert", split_axis=0, concat_axis=0, tiled=True
        ),
        lax.all_to_all(
            sum_dc.reshape(n_expert, cap_rows), "expert", split_axis=0, concat_axis=0, tiled=True
        ),
    )
    grad_tokens = jnp.dot(
        both, back_dx.reshape(width, -1), preferred_element_type=f32
    ).astype(bf16)
    grad_combine = jnp.sum(picks.astype(f32) * back_dc.reshape(width), axis=2)
    return (grad_tokens, grad_combine, grad_w_in[None], grad_b_in[None], grad_w_out[None], grad_b_out[None])


F32, BF16 = jnp.float32, jnp.bfloat16
CORES = 2
LANES = 128


def matmul(left, right, dims):
    return lax.dot_general(left, right, (dims, ((), ())), preferred_element_type=F32)


def split_pair(value, rows):
    high = value.astype(BF16).astype(F32)
    lane = lax.broadcasted_iota(jnp.int32, (rows, LANES), 1)
    return jnp.where(lane < LANES // 2, high, value - high).astype(BF16)


def join_pair(pair):
    return jnp.sum(pair.astype(F32), axis=1, keepdims=True) * (2.0 / LANES)


def fused_kernel(
    n_expert, chips, cap, x_hbm, g_hbm, meta_hbm, w_in_hbm, b_in_ref, w_out_hbm, b_out_ref,
    gt_ref, gc_ref, gwi_hbm, gbi_ref, gwo_hbm, gbo_ref,
    w_in_ref, w_out_ref, gwi_ref, gwo_ref, tok, sendbuf, rows, hid, dpre, dout, dx, dxrecv, retsend, retrecv, fsend, frecv, facc,
    tok_s, tok_r, xy_s, xy_r, sib_s, sib_r, dx_s, dx_r, ret_s, ret_r, fin_s, fin_r, loc,
):
    me_e = lax.axis_index("expert")
    me_z = lax.axis_index("zero")
    chip, core = me_z // CORES, me_z % CORES
    width = n_expert * cap
    toks = tok.shape[1]
    dim = w_in_ref.shape[0]
    units = w_in_ref.shape[1]
    sibling = (me_e, chip * CORES + 1 - core)

    def chunk(index):
        return pl.ds(pl.multiple_of(index * cap, cap), cap)

    def expert_peer(p):
        return lax.rem(me_e + p, n_expert)

    def chip_peer(p):
        return lax.rem(chip + p, chips)

    def order(step):
        low = chip
        high = chips - 1 - chip
        least = jnp.minimum(low, high)
        half = (step + 1) // 2
        near = jnp.where(step % 2 == 1, chip + half, chip - half)
        far = jnp.where(low < high, step, chips - 1 - step)
        return jnp.where(step <= 2 * least, near, far)

    def remote(src, dst, send, recv, device):
        return pltpu.make_async_remote_copy(
            src_ref=src, dst_ref=dst, send_sem=send, recv_sem=recv, device_id=device,
            device_id_type=pl.DeviceIdType.MESH,
        )

    def tok_copy(src, way):
        to = chip + (1 if way else -1)
        return remote(
            tok.at[src], tok.at[src], tok_s.at[way, src], tok_r.at[src],
            (me_e, to * CORES + core),
        )

    def pass_tokens(away):
        @pl.when(chip >= away)
        def _():
            tok_copy(chip - away, 1).wait_recv()

            @pl.when(chip < chips - 1)
            def _():
                tok_copy(chip - away, 1).start()

        @pl.when(chip + away < chips)
        def _():
            tok_copy(chip + away, 0).wait_recv()

            @pl.when(chip > 0)
            def _():
                tok_copy(chip + away, 0).start()

    def xy_copy(src, peer, frm):
        return remote(
            sendbuf.at[src, chunk(peer)], rows.at[src * CORES + core, chunk(frm)],
            xy_s.at[src, peer], xy_r.at[src, frm], (peer, me_z),
        )

    def sib_copy(src, e, lane):
        return remote(
            rows.at[src * CORES + lane, chunk(e)], rows.at[src * CORES + lane, chunk(e)],
            sib_s.at[src, e], sib_r.at[src, e], sibling,
        )

    def dx_copy(src, lane):
        return remote(
            dx.at[src * CORES + lane], dxrecv.at[src], dx_s.at[src], dx_r.at[src], sibling
        )

    def ret_copy(src, peer, frm):
        return remote(
            retsend.at[src, chunk(peer)], retrecv.at[src, chunk(frm)],
            ret_s.at[src, peer], ret_r.at[src, frm], (peer, me_z),
        )

    def fin_copy(to, frm):
        return remote(
            fsend.at[to], frecv.at[frm], fin_s.at[to], fin_r.at[frm], (me_e, to * CORES + core)
        )

    def picks_of(src):
        meta = tok[src, :, 2 * dim :].astype(F32)
        spots = lax.broadcasted_iota(jnp.int32, (toks, width), 1).astype(F32)
        quarter = LANES // 4
        first = jnp.where(meta[:, 0:1] == spots, 1.0, 0.0)
        second = jnp.where(meta[:, quarter : quarter + 1] == spots, 1.0, 0.0)
        return first, second, meta

    def stage_tokens(src):
        first, second, meta = picks_of(src)
        quarter = LANES // 4
        both = (first + second).T.astype(BF16)
        step = 512
        for col in range(0, 2 * dim, step):
            out = matmul(both, tok[src, :, col : col + step], ((1,), (0,)))
            sendbuf[src, :, col : col + step] = out.astype(BF16)
        w0 = jnp.broadcast_to(meta[:, 2 * quarter : 2 * quarter + 1], (toks, LANES)).astype(BF16)
        w1 = jnp.broadcast_to(meta[:, 3 * quarter : 3 * quarter + 1], (toks, LANES)).astype(BF16)
        out = matmul(first.T.astype(BF16), w0, ((1,), (0,))) + matmul(
            second.T.astype(BF16), w1, ((1,), (0,))
        )
        sendbuf[src, :, 2 * dim :] = out.astype(BF16)
        for p in range(1, n_expert):
            xy_copy(src, expert_peer(p), me_e).start()
        rows[src * CORES + core, chunk(me_e), :] = sendbuf[src, chunk(me_e), :]
        sib_copy(src, me_e, core).start()

    def stage_rows(src):
        for p in range(1, n_expert):
            peer = expert_peer(p)
            xy_copy(src, peer, peer).wait_recv()
            sib_copy(src, peer, core).start()
        for e in range(n_expert):
            sib_copy(src, e, 1 - core).wait_recv()

    def stage_compute(src):
        pair = pl.ds(src * CORES, CORES)
        both = CORES * width
        weight = rows[pair, :, 2 * dim :].reshape(both, LANES).astype(F32)[:, 0:1]
        inner = jnp.zeros((both, 1), F32)
        tile = 256
        for col in range(0, units, tile):
            cols = slice(col, col + tile)
            x = rows[pair, :, :dim].reshape(both, dim)
            pre = matmul(x, w_in_ref[:, cols], ((1,), (0,)))
            pre = pre + b_in_ref[:, cols].astype(F32)
            g = rows[pair, :, dim : 2 * dim].reshape(both, dim)
            back = matmul(g, w_out_ref[cols, :], ((1,), (1,)))
            hidden32, slope = gelu_parts(pre)
            inner = inner + jnp.sum(hidden32 * back, axis=1, keepdims=True)
            hid[pair, :, cols] = hidden32.astype(BF16).reshape(CORES, width, tile)
            dpre[pair, :, cols] = (weight * back * slope).astype(BF16).reshape(CORES, width, tile)
        for col in range(0, dim, 512):
            d = dpre[pair].reshape(both, units)
            out = matmul(d, w_in_ref[col : col + 512, :], ((1,), (1,)))
            dx[pair, :, col : col + 512] = out.astype(BF16).reshape(CORES, width, 512)
        dx[pair, :, dim:] = split_pair(inner, both).reshape(CORES, width, LANES)
        dx_copy(src, 1 - core).start()

    def stage_return(src):
        for lane in range(CORES):
            g = src * CORES + lane
            weight = rows[g, :, 2 * dim :].astype(F32)[:, 0:1]
            dout[g] = (weight * rows[g, :, dim : 2 * dim].astype(F32)).astype(BF16)
        g = src * CORES + core
        grads = rows[g, :, dim : 2 * dim].astype(F32)
        bias = jnp.sum(grads * b_out_ref[...].astype(F32), axis=1, keepdims=True)
        bias = bias * jnp.where(src == chip, 1.0, 0.0)
        dx_copy(src, core).wait_recv()
        total = dx[g, :, :dim].astype(F32) + dxrecv[src, :, :dim].astype(F32)
        retsend[src, :, :dim] = total.astype(BF16)
        pair = join_pair(dx[g, :, dim:]) + join_pair(dxrecv[src, :, dim:]) + bias
        retsend[src, :, dim:] = split_pair(pair, width)
        for p in range(1, n_expert):
            ret_copy(src, expert_peer(p), me_e).start()
        retrecv[src, chunk(me_e), :] = retsend[src, chunk(me_e), :]

    def in_halves(one, two):
        lane = lax.broadcasted_iota(jnp.int32, (toks, LANES), 1)
        return jnp.where(lane < LANES // 2, one, two)

    def stage_combine(src):
        for p in range(1, n_expert):
            peer = expert_peer(p)
            ret_copy(src, peer, peer).wait_recv()
        first, second, _ = picks_of(src)
        both = (first + second).astype(BF16)
        grads = matmul(both, retrecv[src, :, :dim], ((1,), (0,)))
        ext = retrecv[src, :, dim:]
        one = join_pair(matmul(first.astype(BF16), ext, ((1,), (0,))))
        two = join_pair(matmul(second.astype(BF16), ext, ((1,), (0,))))

        @pl.when(src == chip)
        def _():
            facc[:, :dim] = grads
            facc[:, dim:] = in_halves(one, two)

        @pl.when(src != chip)
        def _():
            fsend[src, :, :dim] = grads.astype(BF16)
            high = in_halves(one, two).astype(BF16).astype(F32)
            odd = lax.broadcasted_iota(jnp.int32, (toks, LANES), 1) % 2
            ext = jnp.where(odd == 0, high, in_halves(one, two) - high)
            fsend[src, :, dim:] = ext.astype(BF16)
            fin_copy(src, chip).start()

    barrier = pltpu.get_barrier_semaphore()

    def greet(device):
        pl.semaphore_signal(
            barrier, inc=1, device_id=device, device_id_type=pl.DeviceIdType.MESH
        )

    for p in range(1, n_expert):
        greet((expert_peer(p), me_z))
    for p in range(1, chips):
        greet((me_e, chip_peer(p) * CORES + core))
    greet(sibling)
    loads = [
        pltpu.make_async_copy(src, dst, loc.at[i])
        for i, (src, dst) in enumerate((
            (x_hbm, tok.at[chip, :, :dim]),
            (g_hbm, tok.at[chip, :, dim : 2 * dim]),
            (meta_hbm, tok.at[chip, :, 2 * dim :]),
            (w_in_hbm, w_in_ref),
            (w_out_hbm, w_out_ref),
        ))
    ]
    for load in loads:
        load.start()
    for load in loads[:3]:
        load.wait()
    pl.semaphore_wait(barrier, n_expert + chips - 1)

    @pl.when(chip < chips - 1)
    def _():
        tok_copy(chip, 1).start()

    @pl.when(chip > 0)
    def _():
        tok_copy(chip, 0).start()

    @pl.loop(0, chips + 1)
    def _(step):
        @pl.when((step >= 1) & (step < chips))
        def _():
            pass_tokens(step)

        @pl.when(step < chips)
        def _():
            stage_tokens(order(step))

        @pl.when(step == 0)
        def _():
            for load in loads[3:]:
                load.wait()

        @pl.when(step >= 1)
        def _():
            stage_rows(order(step - 1))
            stage_compute(order(step - 1))
            stage_return(order(step - 1))

        @pl.when(step >= 2)
        def _():
            stage_combine(order(step - 2))

    groups = chips * CORES
    all_rows = groups * width

    def weights_in(first, last):
        for col in range(first, last, 256):
            x_all = rows[:, :, col : col + 256].reshape(all_rows, 256)
            d_all = dpre[...].reshape(all_rows, units)
            gwi_ref[col : col + 256, :] = matmul(x_all, d_all, ((0,), (0,))).astype(BF16)

    weights_in(0, dim // 2)
    stage_combine(order(chips - 1))
    weights_in(dim // 2, dim)
    store_in = pltpu.make_async_copy(gwi_ref, gwi_hbm, loc.at[5])
    store_in.start()
    o_all = dout[...].reshape(all_rows, dim)
    for col in range(0, units, 256):
        h_all = hid[:, :, col : col + 256].reshape(all_rows, 256)
        gwo_ref[col : col + 256, :] = matmul(h_all, o_all, ((0,), (0,))).astype(BF16)
    store_out = pltpu.make_async_copy(gwo_ref, gwo_hbm, loc.at[6])
    store_out.start()
    ones = jnp.ones((8, all_rows), BF16)
    gbi_ref[...] = matmul(ones, dpre[...].reshape(all_rows, units), ((1,), (0,)))[0:1]
    gbo_ref[...] = matmul(ones, o_all, ((1,), (0,)))[0:1]

    total = facc[:, :dim]
    ext = facc[:, dim:]
    one, two = ext[:, 0:1], ext[:, LANES // 2 : LANES // 2 + 1]
    lane = lax.broadcasted_iota(jnp.int32, (toks, LANES), 1)
    for p in range(1, chips):
        other = chip_peer(p)
        fin_copy(other, other).wait_recv()
        total = total + frecv[other, :, :dim].astype(F32)
        ext = frecv[other, :, dim:].astype(F32)
        scale = 4.0 / LANES
        one = one + scale * jnp.sum(
            jnp.where(lane < LANES // 2, ext, 0.0), axis=1, keepdims=True
        )
        two = two + scale * jnp.sum(
            jnp.where(lane < LANES // 2, 0.0, ext), axis=1, keepdims=True
        )
    gt_ref[...] = total.astype(BF16)
    gc_ref[:, 0:1] = one
    gc_ref[:, 1:2] = two
    store_in.wait()
    store_out.wait()

    for p in range(1, chips):
        other = chip_peer(p)
        fin_copy(other, chip).wait_send()
    for src in range(chips):
        @pl.when((src <= chip) & (chip < chips - 1))
        def _():
            tok_copy(src, 1).wait_send()

        @pl.when((src >= chip) & (chip > 0))
        def _():
            tok_copy(src, 0).wait_send()

        for p in range(1, n_expert):
            xy_copy(src, expert_peer(p), me_e).wait_send()
            ret_copy(src, expert_peer(p), me_e).wait_send()
        for e in range(n_expert):
            sib_copy(src, e, core).wait_send()
        dx_copy(src, 1 - core).wait_send()


def hand_over(a_in, b_in, c_in, a_out, b_out, c_out, sems):
    copies = []
    for i, (src, dst) in enumerate(((a_in, a_out), (b_in, b_out), (c_in, c_out))):
        part = src.shape[0] // 4
        for j in range(4):
            at = pl.ds(j * part, part)
            copies.append(pltpu.make_async_copy(src.at[at], dst.at[at], sems.at[4 * i + j]))
    for copy in copies:
        copy.start()
    for copy in copies:
        copy.wait()


def scratch_sizes(n_expert, chips, cap, toks, dim, units):
    width, groups = n_expert * cap, chips * CORES
    return [
        ((dim, units), BF16),
        ((units, dim), BF16),
        ((dim, units), BF16),
        ((units, dim), BF16),
        ((chips, toks, 2 * dim + LANES), BF16),
        ((chips, width, 2 * dim + LANES), BF16),
        ((groups, width, 2 * dim + LANES), BF16),
        ((groups, width, units), BF16),
        ((groups, width, units), BF16),
        ((groups, width, dim), BF16),
        ((groups, width, dim + LANES), BF16),
        ((chips, width, dim + LANES), BF16),
        ((chips, width, dim + LANES), BF16),
        ((chips, width, dim + LANES), BF16),
        ((chips, toks, dim + LANES), BF16),
        ((chips, toks, dim + LANES), BF16),
        ((toks, dim + LANES), F32),
    ]


def on_device(tokens, grads_out, routes, slots, combine, w_in, b_in, w_out, b_out):
    n_expert = lax.axis_size("expert")
    n_zero = lax.axis_size("zero")
    toks, dim = tokens.shape
    units = w_in.shape[2]
    cap = TOP * toks // n_expert
    chips = n_zero // CORES
    sizes = scratch_sizes(n_expert, chips, cap, toks, dim, units)
    held = sum(functools.reduce(lambda a, b: a * b, s) * jnp.dtype(t).itemsize for s, t in sizes)
    if held > (46 << 20) or n_expert * cap > 256 or n_zero % CORES or chips < 3:
        return plain_device(
            tokens, grads_out, routes, slots, combine, w_in, b_in, w_out, b_out
        )
    places = jnp.where(slots < cap, routes * cap + slots, -1).astype(BF16)
    meta = jnp.repeat(jnp.concatenate([places, combine], axis=1), LANES // 4, axis=1)
    vmem = pl.BlockSpec(memory_space=pltpu.VMEM)
    hbm = pl.BlockSpec(memory_space=pl.ANY)
    sem = pltpu.SemaphoreType.DMA
    outs = pl.pallas_call(
        functools.partial(fused_kernel, n_expert, chips, cap),
        out_shape=(
            jax.ShapeDtypeStruct((toks, dim), BF16),
            jax.ShapeDtypeStruct((toks, TOP), F32),
            jax.ShapeDtypeStruct((dim, units), BF16),
            jax.ShapeDtypeStruct((1, units), F32),
            jax.ShapeDtypeStruct((units, dim), BF16),
            jax.ShapeDtypeStruct((1, dim), F32),
        ),
        in_specs=[hbm, hbm, hbm, hbm, vmem, hbm, vmem],
        out_specs=(vmem, vmem, hbm, vmem, hbm, vmem),
        scratch_shapes=[pltpu.VMEM(s, t) for s, t in sizes]
        + [
            sem((2, chips)), sem((chips,)),
            sem((chips, n_expert)), sem((chips, n_expert)),
            sem((chips, n_expert)), sem((chips, n_expert)),
            sem((chips,)), sem((chips,)),
            sem((chips, n_expert)), sem((chips, n_expert)),
            sem((chips,)), sem((chips,)),
            sem((7,)),
        ],
        compiler_params=pltpu.CompilerParams(
            collective_id=0, has_side_effects=True, vmem_limit_bytes=60 << 20
        ),
        name="routed_expert_backward",
    )(tokens, grads_out, meta, w_in[0], b_in, w_out[0], b_out)
    gt, gc, gwi, gbi, gwo, gbo = outs
    gt, gwi, gwo = pl.pallas_call(
        hand_over,
        out_shape=tuple(jax.ShapeDtypeStruct(a.shape, a.dtype) for a in (gt, gwi, gwo)),
        in_specs=[hbm] * 3,
        out_specs=(hbm,) * 3,
        scratch_shapes=[sem((12,))],
        compiler_params=pltpu.CompilerParams(vmem_limit_bytes=60 << 20),
        name="hand_over",
    )(gt, gwi, gwo)
    return (gt, gc, gwi[None], gbi, gwo[None], gbo)


def solution(mesh):
    in_specs = (
        P(("expert", "zero"), None),
        P(("expert", "zero"), None),
        P(("expert", "zero"), None),
        P(("expert", "zero"), None),
        P(("expert", "zero"), None),
        P("expert", None, "zero"),
        P("expert", "zero"),
        P("expert", "zero", None),
        P("expert", None),
    )
    out_specs = (
        P(("expert", "zero"), None),
        P(("expert", "zero"), None),
        P("expert", None, "zero"),
        P("expert", "zero"),
        P("expert", "zero", None),
        P("expert", None),
    )
    return jax.shard_map(
        on_device, mesh=mesh, in_specs=in_specs, out_specs=out_specs, check_vma=False
    )
```

```python
import functools

import jax
import jax.numpy as jnp
from jax import lax
from jax.experimental import pallas as pl
from jax.experimental.pallas import tpu as pltpu
from jax.sharding import PartitionSpec as P

TOP = 2


def gelu_parts(pre):
    cdf = 0.5 * (1.0 + lax.erf(pre * 0.7071067811865476))
    dens = jnp.exp(-0.5 * pre * pre) * 0.3989422804014327
    return (pre * cdf, cdf + pre * dens)


def plain_device(tokens, grads_out, routes, slots, combine, w_in, b_in, w_out, b_out):
    f32, bf16 = jnp.float32, jnp.bfloat16
    n_expert = lax.axis_size("expert")
    n_zero = lax.axis_size("zero")
    tok_rows, dim = tokens.shape
    cap_rows = TOP * tok_rows // n_expert
    width = n_expert * cap_rows
    spots = jnp.arange(width, dtype=jnp.int32)
    places = jnp.where(slots < cap_rows, routes * cap_rows + slots, -1)
    picks = (places[:, :, None] == spots[None, None, :]).astype(bf16)
    both = picks[:, 0] + picks[:, 1]
    pair = jnp.concatenate([tokens, grads_out], axis=1)
    send = jnp.einsum("tp,td->pd", both, pair, preferred_element_type=f32).astype(bf16)
    send_c = jnp.einsum("tkp,tk->p", picks, combine, preferred_element_type=f32).astype(bf16)
    send = jnp.concatenate([send, jnp.broadcast_to(send_c[:, None], (width, 128))], axis=1)
    got = lax.all_to_all(
        send.reshape(n_expert, cap_rows, -1), "expert", split_axis=0, concat_axis=0, tiled=True
    ).reshape(width, -1)
    rows = lax.all_gather(got, "zero", axis=0, tiled=True)
    rows_x = rows[:, :dim]
    rows_g = rows[:, dim : 2 * dim]
    weight = rows[:, 2 * dim : 2 * dim + 1].astype(f32)
    pre = jnp.dot(rows_x, w_in[0], preferred_element_type=f32) + b_in.astype(f32)
    hidden32, slope = gelu_parts(pre)
    back = jnp.einsum("rd,fd->rf", rows_g, w_out[0], preferred_element_type=f32)
    inner = jnp.sum(hidden32 * back, axis=1)
    hidden = hidden32.astype(bf16)
    dpre = (weight * back * slope).astype(bf16)
    dout = (weight * rows_g.astype(f32)).astype(bf16)
    slot_dx = jnp.einsum("rf,df->rd", dpre, w_in[0], preferred_element_type=f32).astype(bf16)
    part_dx = lax.all_to_all(
        slot_dx.reshape(n_zero, width, dim), "zero", split_axis=0, concat_axis=0, tiled=True
    )
    sum_dx = jnp.sum(part_dx.astype(f32), axis=0).astype(bf16)
    part_dc = lax.all_to_all(
        inner.reshape(n_zero, width), "zero", split_axis=0, concat_axis=0, tiled=True
    )
    bias_dc = jnp.sum(got[:, dim : 2 * dim].astype(f32) * b_out.astype(f32), axis=1)
    sum_dc = jnp.sum(part_dc, axis=0) + bias_dc
    grad_w_in = jnp.einsum("ra,rb->ab", rows_x, dpre, preferred_element_type=f32).astype(bf16)
    grad_w_out = jnp.einsum("ra,rb->ab", hidden, dout, preferred_element_type=f32).astype(bf16)
    grad_b_in = jnp.sum(dpre.astype(f32), axis=0)
    grad_b_out = jnp.sum(dout.astype(f32), axis=0)
    back_dx, back_dc = (
        lax.all_to_all(
            sum_dx.reshape(n_expert, cap_rows, -1), "expert", split_axis=0, concat_axis=0, tiled=True
        ),
        lax.all_to_all(
            sum_dc.reshape(n_expert, cap_rows), "expert", split_axis=0, concat_axis=0, tiled=True
        ),
    )
    grad_tokens = jnp.dot(
        both, back_dx.reshape(width, -1), preferred_element_type=f32
    ).astype(bf16)
    grad_combine = jnp.sum(picks.astype(f32) * back_dc.reshape(width), axis=2)
    return (grad_tokens, grad_combine, grad_w_in[None], grad_b_in[None], grad_w_out[None], grad_b_out[None])


F32, BF16 = jnp.float32, jnp.bfloat16
CORES = 2
LANES = 128


def matmul(left, right, dims):
    return lax.dot_general(left, right, (dims, ((), ())), preferred_element_type=F32)


def split_pair(value, rows):
    high = value.astype(BF16).astype(F32)
    lane = lax.broadcasted_iota(jnp.int32, (rows, LANES), 1)
    return jnp.where(lane < LANES // 2, high, value - high).astype(BF16)


def join_pair(pair):
    return jnp.sum(pair.astype(F32), axis=1, keepdims=True) * (2.0 / LANES)


def fused_kernel(
    n_expert, chips, cap, x_hbm, g_hbm, meta_hbm, w_in_hbm, b_in_ref, w_out_hbm, b_out_ref,
    gt_ref, gc_ref, gwi_hbm, gbi_ref, gwo_hbm, gbo_ref,
    w_in_ref, w_out_ref, gwi_ref, gwo_ref, tok, sendbuf, rows, hid, dpre, dout, dx, dxrecv, retsend, retrecv, fsend, frecv, facc,
    tok_s, tok_r, xy_s, xy_r, sib_s, sib_r, dx_s, dx_r, ret_s, ret_r, fin_s, fin_r, loc, part, part_sem,
):
    me_e = lax.axis_index("expert")
    me_z = lax.axis_index("zero")
    chip, core = me_z // CORES, me_z % CORES
    width = n_expert * cap
    toks = tok.shape[1]
    dim = w_in_ref.shape[0]
    units = w_in_ref.shape[1]
    sibling = (me_e, chip * CORES + 1 - core)

    def chunk(index):
        return pl.ds(pl.multiple_of(index * cap, cap), cap)

    def expert_peer(p):
        return lax.rem(me_e + p, n_expert)

    def chip_peer(p):
        return lax.rem(chip + p, chips)

    partner = chip + 1 - 2 * (chip % 2)
    base = chips // 2 * (1 - chip // 2)

    def order(step):
        far = jnp.where(chip < chips // 2, step, chips - 1 - step)
        return jnp.where(step == 0, chip, jnp.where(step == 1, partner, far))

    def remote(src, dst, send, recv, device):
        return pltpu.make_async_remote_copy(
            src_ref=src, dst_ref=dst, send_sem=send, recv_sem=recv, device_id=device,
            device_id_type=pl.DeviceIdType.MESH,
        )

    def tok_copy(src, way):
        to = chip + (1 if way else -1)
        return remote(
            tok.at[src], tok.at[src], tok_s.at[way, src], tok_r.at[src],
            (me_e, to * CORES + core),
        )

    def pass_tokens(away):
        @pl.when(chip >= away)
        def _():
            tok_copy(chip - away, 1).wait_recv()

            @pl.when(chip < chips - 1)
            def _():
                tok_copy(chip - away, 1).start()

        @pl.when(chip + away < chips)
        def _():
            tok_copy(chip + away, 0).wait_recv()

            @pl.when(chip > 0)
            def _():
                tok_copy(chip + away, 0).start()

    def xy_copy(src, peer, frm):
        return remote(
            sendbuf.at[src, chunk(peer)], rows.at[src * CORES + core, chunk(frm)],
            xy_s.at[src, peer], xy_r.at[src, frm], (peer, me_z),
        )

    def sib_copy(src, e, lane):
        return remote(
            rows.at[src * CORES + lane, chunk(e)], rows.at[src * CORES + lane, chunk(e)],
            sib_s.at[src, e], sib_r.at[src, e], sibling,
        )

    def dx_copy(src, lane):
        return remote(
            dx.at[src * CORES + lane], dxrecv.at[src], dx_s.at[src], dx_r.at[src], sibling
        )

    def ret_copy(src, peer, frm):
        return remote(
            retsend.at[src, chunk(peer)], retrecv.at[src, chunk(frm)],
            ret_s.at[src, peer], ret_r.at[src, frm], (peer, me_z),
        )

    def part_copy():
        return remote(
            retsend.at[partner], part, part_sem.at[0], part_sem.at[1],
            (me_e, partner * CORES + core),
        )

    def fin_copy(to, frm):
        return remote(
            fsend.at[to], frecv.at[frm], fin_s.at[to], fin_r.at[frm], (me_e, to * CORES + core)
        )

    def picks_of(src):
        meta = tok[src, :, 2 * dim :].astype(F32)
        spots = lax.broadcasted_iota(jnp.int32, (toks, width), 1).astype(F32)
        quarter = LANES // 4
        first = jnp.where(meta[:, 0:1] == spots, 1.0, 0.0)
        second = jnp.where(meta[:, quarter : quarter + 1] == spots, 1.0, 0.0)
        return first, second, meta

    def stage_tokens(src):
        first, second, meta = picks_of(src)
        quarter = LANES // 4
        both = (first + second).T.astype(BF16)
        step = 512
        for col in range(0, 2 * dim, step):
            out = matmul(both, tok[src, :, col : col + step], ((1,), (0,)))
            sendbuf[src, :, col : col + step] = out.astype(BF16)
        w0 = jnp.broadcast_to(meta[:, 2 * quarter : 2 * quarter + 1], (toks, LANES)).astype(BF16)
        w1 = jnp.broadcast_to(meta[:, 3 * quarter : 3 * quarter + 1], (toks, LANES)).astype(BF16)
        out = matmul(first.T.astype(BF16), w0, ((1,), (0,))) + matmul(
            second.T.astype(BF16), w1, ((1,), (0,))
        )
        sendbuf[src, :, 2 * dim :] = out.astype(BF16)
        for p in range(1, n_expert):
            xy_copy(src, expert_peer(p), me_e).start()
        rows[src * CORES + core, chunk(me_e), :] = sendbuf[src, chunk(me_e), :]
        sib_copy(src, me_e, core).start()

    def stage_rows(src):
        for p in range(1, n_expert):
            peer = expert_peer(p)
            xy_copy(src, peer, peer).wait_recv()
            sib_copy(src, peer, core).start()
        for e in range(n_expert):
            sib_copy(src, e, 1 - core).wait_recv()

    def stage_compute(src):
        pair = pl.ds(src * CORES, CORES)
        both = CORES * width
        weight = rows[pair, :, 2 * dim :].reshape(both, LANES).astype(F32)[:, 0:1]
        inner = jnp.zeros((both, 1), F32)
        tile = 256
        for col in range(0, units, tile):
            cols = slice(col, col + tile)
            x = rows[pair, :, :dim].reshape(both, dim)
            pre = matmul(x, w_in_ref[:, cols], ((1,), (0,)))
            pre = pre + b_in_ref[:, cols].astype(F32)
            g = rows[pair, :, dim : 2 * dim].reshape(both, dim)
            back = matmul(g, w_out_ref[cols, :], ((1,), (1,)))
            hidden32, slope = gelu_parts(pre)
            inner = inner + jnp.sum(hidden32 * back, axis=1, keepdims=True)
            hid[pair, :, cols] = hidden32.astype(BF16).reshape(CORES, width, tile)
            dpre[pair, :, cols] = (weight * back * slope).astype(BF16).reshape(CORES, width, tile)
        for col in range(0, dim, 512):
            d = dpre[pair].reshape(both, units)
            out = matmul(d, w_in_ref[col : col + 512, :], ((1,), (1,)))
            dx[pair, :, col : col + 512] = out.astype(BF16).reshape(CORES, width, 512)
        dx[pair, :, dim:] = split_pair(inner, both).reshape(CORES, width, LANES)
        dx_copy(src, 1 - core).start()

    def send_return(src):
        for p in range(1, n_expert):
            ret_copy(src, expert_peer(p), me_e).start()
        retrecv[src, chunk(me_e), :] = retsend[src, chunk(me_e), :]

    def return_own():
        part_copy().wait_recv()
        total = retsend[chip, :, :dim].astype(F32) + part[:, :dim].astype(F32)
        retsend[chip, :, :dim] = total.astype(BF16)
        pair = join_pair(retsend[chip, :, dim:]) + join_pair(part[:, dim:])
        retsend[chip, :, dim:] = split_pair(pair, width)
        send_return(chip)

    def stage_return(src):
        for lane in range(CORES):
            g = src * CORES + lane
            weight = rows[g, :, 2 * dim :].astype(F32)[:, 0:1]
            dout[g] = (weight * rows[g, :, dim : 2 * dim].astype(F32)).astype(BF16)
        g = src * CORES + core
        grads = rows[g, :, dim : 2 * dim].astype(F32)
        bias = jnp.sum(grads * b_out_ref[...].astype(F32), axis=1, keepdims=True)
        bias = bias * jnp.where(src == chip, 1.0, 0.0)
        dx_copy(src, core).wait_recv()
        total = dx[g, :, :dim].astype(F32) + dxrecv[src, :, :dim].astype(F32)
        retsend[src, :, :dim] = total.astype(BF16)
        pair = join_pair(dx[g, :, dim:]) + join_pair(dxrecv[src, :, dim:]) + bias
        retsend[src, :, dim:] = split_pair(pair, width)

        @pl.when(src == partner)
        def _():
            part_copy().start()

        @pl.when((src != partner) & (src != chip))
        def _():
            send_return(src)

    def in_halves(one, two):
        lane = lax.broadcasted_iota(jnp.int32, (toks, LANES), 1)
        return jnp.where(lane < LANES // 2, one, two)

    def stage_combine(src):
        for p in range(1, n_expert):
            peer = expert_peer(p)
            ret_copy(src, peer, peer).wait_recv()
        first, second, _ = picks_of(src)
        both = (first + second).astype(BF16)
        grads = matmul(both, retrecv[src, :, :dim], ((1,), (0,)))
        ext = retrecv[src, :, dim:]
        one = join_pair(matmul(first.astype(BF16), ext, ((1,), (0,))))
        two = join_pair(matmul(second.astype(BF16), ext, ((1,), (0,))))

        @pl.when(src == chip)
        def _():
            facc[:, :dim] = grads
            facc[:, dim:] = in_halves(one, two)

        @pl.when(src != chip)
        def _():
            fsend[src, :, :dim] = grads.astype(BF16)
            high = in_halves(one, two).astype(BF16).astype(F32)
            odd = lax.broadcasted_iota(jnp.int32, (toks, LANES), 1) % 2
            ext = jnp.where(odd == 0, high, in_halves(one, two) - high)
            fsend[src, :, dim:] = ext.astype(BF16)
            fin_copy(src, chip).start()

    barrier = pltpu.get_barrier_semaphore()

    def greet(device):
        pl.semaphore_signal(
            barrier, inc=1, device_id=device, device_id_type=pl.DeviceIdType.MESH
        )

    for p in range(1, n_expert):
        greet((expert_peer(p), me_z))
    for p in range(1, chips):
        greet((me_e, chip_peer(p) * CORES + core))
    greet(sibling)
    loads = [
        pltpu.make_async_copy(src, dst, loc.at[i])
        for i, (src, dst) in enumerate((
            (x_hbm, tok.at[chip, :, :dim]),
            (g_hbm, tok.at[chip, :, dim : 2 * dim]),
            (meta_hbm, tok.at[chip, :, 2 * dim :]),
            (w_in_hbm, w_in_ref),
            (w_out_hbm, w_out_ref),
        ))
    ]
    for load in loads:
        load.start()
    for load in loads[:3]:
        load.wait()
    pl.semaphore_wait(barrier, n_expert + chips - 1)

    @pl.when(chip < chips - 1)
    def _():
        tok_copy(chip, 1).start()

    @pl.when(chip > 0)
    def _():
        tok_copy(chip, 0).start()

    @pl.loop(0, chips + 1)
    def _(step):
        @pl.when((step >= 1) & (step < chips))
        def _():
            pass_tokens(step)

        @pl.when(step < chips)
        def _():
            stage_tokens(order(step))

        @pl.when(step == 0)
        def _():
            for load in loads[3:]:
                load.wait()

        @pl.when(step >= 1)
        def _():
            stage_rows(order(step - 1))

        @pl.when(step == chips)
        def _():
            return_own()

        @pl.when(step >= 1)
        def _():
            stage_compute(order(step - 1))
            stage_return(order(step - 1))

        @pl.when(step == chips)
        def _():
            stage_combine(order(step - 2))

    groups = chips * CORES
    all_rows = groups * width

    def weights_in(first, last):
        for col in range(first, last, 256):
            x_all = rows[:, :, col : col + 256].reshape(all_rows, 256)
            d_all = dpre[...].reshape(all_rows, units)
            gwi_ref[col : col + 256, :] = matmul(x_all, d_all, ((0,), (0,))).astype(BF16)

    weights_in(0, dim // 2)
    stage_combine(order(chips - 1))
    stage_combine(chip)
    weights_in(dim // 2, dim)
    store_in = pltpu.make_async_copy(gwi_ref, gwi_hbm, loc.at[5])
    store_in.start()
    o_all = dout[...].reshape(all_rows, dim)
    for col in range(0, units, 256):
        h_all = hid[:, :, col : col + 256].reshape(all_rows, 256)
        gwo_ref[col : col + 256, :] = matmul(h_all, o_all, ((0,), (0,))).astype(BF16)
    store_out = pltpu.make_async_copy(gwo_ref, gwo_hbm, loc.at[6])
    store_out.start()
    ones = jnp.ones((8, all_rows), BF16)
    gbi_ref[...] = matmul(ones, dpre[...].reshape(all_rows, units), ((1,), (0,)))[0:1]
    gbo_ref[...] = matmul(ones, o_all, ((1,), (0,)))[0:1]

    total = facc[:, :dim]
    ext = facc[:, dim:]
    one, two = ext[:, 0:1], ext[:, LANES // 2 : LANES // 2 + 1]
    lane = lax.broadcasted_iota(jnp.int32, (toks, LANES), 1)
    for p in range(chips // 2):
        other = base + p
        fin_copy(other, other).wait_recv()
        total = total + frecv[other, :, :dim].astype(F32)
        ext = frecv[other, :, dim:].astype(F32)
        scale = 4.0 / LANES
        one = one + scale * jnp.sum(
            jnp.where(lane < LANES // 2, ext, 0.0), axis=1, keepdims=True
        )
        two = two + scale * jnp.sum(
            jnp.where(lane < LANES // 2, 0.0, ext), axis=1, keepdims=True
        )
    gt_ref[...] = total.astype(BF16)
    gc_ref[:, 0:1] = one
    gc_ref[:, 1:2] = two
    store_in.wait()
    store_out.wait()

    part_copy().wait_send()
    for p in range(chips // 2):
        fin_copy(base + p, chip).wait_send()
    for src in range(chips):
        @pl.when((src <= chip) & (chip < chips - 1))
        def _():
            tok_copy(src, 1).wait_send()

        @pl.when((src >= chip) & (chip > 0))
        def _():
            tok_copy(src, 0).wait_send()

        for p in range(1, n_expert):
            xy_copy(src, expert_peer(p), me_e).wait_send()

        @pl.when(src != partner)
        def _():
            for p in range(1, n_expert):
                ret_copy(src, expert_peer(p), me_e).wait_send()

        for e in range(n_expert):
            sib_copy(src, e, core).wait_send()
        dx_copy(src, 1 - core).wait_send()


def hand_over(a_in, b_in, c_in, a_out, b_out, c_out, a_mid, b_mid, c_mid, sems):
    loads, stores = [], []
    for i, (src, mid, dst) in enumerate(
        ((b_in, b_mid, b_out), (c_in, c_mid, c_out), (a_in, a_mid, a_out))
    ):
        part = src.shape[0] // 2
        for j in range(2):
            at, k = pl.ds(j * part, part), 2 * i + j
            loads.append(pltpu.make_async_copy(src.at[at], mid.at[at], sems.at[0, k]))
            stores.append(pltpu.make_async_copy(mid.at[at], dst.at[at], sems.at[1, k]))
    for load in loads:
        load.start()
    for load, store in zip(loads, stores):
        load.wait()
        store.start()
    for store in stores:
        store.wait()


def scratch_sizes(n_expert, chips, cap, toks, dim, units):
    width, groups = n_expert * cap, chips * CORES
    return [
        ((dim, units), BF16),
        ((units, dim), BF16),
        ((dim, units), BF16),
        ((units, dim), BF16),
        ((chips, toks, 2 * dim + LANES), BF16),
        ((chips, width, 2 * dim + LANES), BF16),
        ((groups, width, 2 * dim + LANES), BF16),
        ((groups, width, units), BF16),
        ((groups, width, units), BF16),
        ((groups, width, dim), BF16),
        ((groups, width, dim + LANES), BF16),
        ((chips, width, dim + LANES), BF16),
        ((chips, width, dim + LANES), BF16),
        ((chips, width, dim + LANES), BF16),
        ((chips, toks, dim + LANES), BF16),
        ((chips, toks, dim + LANES), BF16),
        ((toks, dim + LANES), F32),
    ]


def on_device(tokens, grads_out, routes, slots, combine, w_in, b_in, w_out, b_out):
    n_expert = lax.axis_size("expert")
    n_zero = lax.axis_size("zero")
    toks, dim = tokens.shape
    units = w_in.shape[2]
    cap = TOP * toks // n_expert
    chips = n_zero // CORES
    sizes = scratch_sizes(n_expert, chips, cap, toks, dim, units)
    held = sum(functools.reduce(lambda a, b: a * b, s) * jnp.dtype(t).itemsize for s, t in sizes)
    if held > (46 << 20) or n_expert * cap > 256 or n_zero % CORES or chips != 4:
        return plain_device(
            tokens, grads_out, routes, slots, combine, w_in, b_in, w_out, b_out
        )
    places = jnp.where(slots < cap, routes * cap + slots, -1).astype(BF16)
    meta = jnp.repeat(jnp.concatenate([places, combine], axis=1), LANES // 4, axis=1)
    vmem = pl.BlockSpec(memory_space=pltpu.VMEM)
    hbm = pl.BlockSpec(memory_space=pl.ANY)
    sem = pltpu.SemaphoreType.DMA
    outs = pl.pallas_call(
        functools.partial(fused_kernel, n_expert, chips, cap),
        out_shape=(
            jax.ShapeDtypeStruct((toks, dim), BF16),
            jax.ShapeDtypeStruct((toks, TOP), F32),
            jax.ShapeDtypeStruct((dim, units), BF16),
            jax.ShapeDtypeStruct((1, units), F32),
            jax.ShapeDtypeStruct((units, dim), BF16),
            jax.ShapeDtypeStruct((1, dim), F32),
        ),
        in_specs=[hbm, hbm, hbm, hbm, vmem, hbm, vmem],
        out_specs=(vmem, vmem, hbm, vmem, hbm, vmem),
        scratch_shapes=[pltpu.VMEM(s, t) for s, t in sizes]
        + [
            sem((2, chips)), sem((chips,)),
            sem((chips, n_expert)), sem((chips, n_expert)),
            sem((chips, n_expert)), sem((chips, n_expert)),
            sem((chips,)), sem((chips,)),
            sem((chips, n_expert)), sem((chips, n_expert)),
            sem((chips,)), sem((chips,)),
            sem((7,)),
            pltpu.VMEM((n_expert * cap, dim + LANES), BF16),
            sem((2,)),
        ],
        compiler_params=pltpu.CompilerParams(
            collective_id=0, has_side_effects=True, vmem_limit_bytes=60 << 20
        ),
        name="routed_expert_backward",
    )(tokens, grads_out, meta, w_in[0], b_in, w_out[0], b_out)
    gt, gc, gwi, gbi, gwo, gbo = outs
    gt, gwi, gwo = pl.pallas_call(
        hand_over,
        out_shape=tuple(jax.ShapeDtypeStruct(a.shape, a.dtype) for a in (gt, gwi, gwo)),
        in_specs=[hbm] * 3,
        out_specs=(hbm,) * 3,
        scratch_shapes=[pltpu.VMEM(a.shape, a.dtype) for a in (gt, gwi, gwo)] + [sem((2, 6))],
        compiler_params=pltpu.CompilerParams(vmem_limit_bytes=60 << 20),
        name="hand_over",
    )(gt, gwi, gwo)
    return (gt, gc, gwi[None], gbi, gwo[None], gbo)


def solution(mesh):
    in_specs = (
        P(("expert", "zero"), None),
        P(("expert", "zero"), None),
        P(("expert", "zero"), None),
        P(("expert", "zero"), None),
        P(("expert", "zero"), None),
        P("expert", None, "zero"),
        P("expert", "zero"),
        P("expert", "zero", None),
        P("expert", None),
    )
    out_specs = (
        P(("expert", "zero"), None),
        P(("expert", "zero"), None),
        P("expert", None, "zero"),
        P("expert", "zero"),
        P("expert", "zero", None),
        P("expert", None),
    )
    return jax.shard_map(
        on_device, mesh=mesh, in_specs=in_specs, out_specs=out_specs, check_vma=False
    )
```

```python
import functools

import jax
import jax.numpy as jnp
from jax import lax
from jax.experimental import pallas as pl
from jax.experimental.pallas import tpu as pltpu
from jax.sharding import PartitionSpec as P

TOP = 2


def gelu_parts(pre):
    cdf = 0.5 * (1.0 + lax.erf(pre * 0.7071067811865476))
    dens = jnp.exp(-0.5 * pre * pre) * 0.3989422804014327
    return (pre * cdf, cdf + pre * dens)


def plain_device(tokens, grads_out, routes, slots, combine, w_in, b_in, w_out, b_out):
    f32, bf16 = jnp.float32, jnp.bfloat16
    n_expert = lax.axis_size("expert")
    n_zero = lax.axis_size("zero")
    tok_rows, dim = tokens.shape
    cap_rows = TOP * tok_rows // n_expert
    width = n_expert * cap_rows
    spots = jnp.arange(width, dtype=jnp.int32)
    places = jnp.where(slots < cap_rows, routes * cap_rows + slots, -1)
    picks = (places[:, :, None] == spots[None, None, :]).astype(bf16)
    both = picks[:, 0] + picks[:, 1]
    pair = jnp.concatenate([tokens, grads_out], axis=1)
    send = jnp.einsum("tp,td->pd", both, pair, preferred_element_type=f32).astype(bf16)
    send_c = jnp.einsum("tkp,tk->p", picks, combine, preferred_element_type=f32).astype(bf16)
    send = jnp.concatenate([send, jnp.broadcast_to(send_c[:, None], (width, 128))], axis=1)
    got = lax.all_to_all(
        send.reshape(n_expert, cap_rows, -1), "expert", split_axis=0, concat_axis=0, tiled=True
    ).reshape(width, -1)
    rows = lax.all_gather(got, "zero", axis=0, tiled=True)
    rows_x = rows[:, :dim]
    rows_g = rows[:, dim : 2 * dim]
    weight = rows[:, 2 * dim : 2 * dim + 1].astype(f32)
    pre = jnp.dot(rows_x, w_in[0], preferred_element_type=f32) + b_in.astype(f32)
    hidden32, slope = gelu_parts(pre)
    back = jnp.einsum("rd,fd->rf", rows_g, w_out[0], preferred_element_type=f32)
    inner = jnp.sum(hidden32 * back, axis=1)
    hidden = hidden32.astype(bf16)
    dpre = (weight * back * slope).astype(bf16)
    dout = (weight * rows_g.astype(f32)).astype(bf16)
    slot_dx = jnp.einsum("rf,df->rd", dpre, w_in[0], preferred_element_type=f32).astype(bf16)
    part_dx = lax.all_to_all(
        slot_dx.reshape(n_zero, width, dim), "zero", split_axis=0, concat_axis=0, tiled=True
    )
    sum_dx = jnp.sum(part_dx.astype(f32), axis=0).astype(bf16)
    part_dc = lax.all_to_all(
        inner.reshape(n_zero, width), "zero", split_axis=0, concat_axis=0, tiled=True
    )
    bias_dc = jnp.sum(got[:, dim : 2 * dim].astype(f32) * b_out.astype(f32), axis=1)
    sum_dc = jnp.sum(part_dc, axis=0) + bias_dc
    grad_w_in = jnp.einsum("ra,rb->ab", rows_x, dpre, preferred_element_type=f32).astype(bf16)
    grad_w_out = jnp.einsum("ra,rb->ab", hidden, dout, preferred_element_type=f32).astype(bf16)
    grad_b_in = jnp.sum(dpre.astype(f32), axis=0)
    grad_b_out = jnp.sum(dout.astype(f32), axis=0)
    back_dx, back_dc = (
        lax.all_to_all(
            sum_dx.reshape(n_expert, cap_rows, -1), "expert", split_axis=0, concat_axis=0, tiled=True
        ),
        lax.all_to_all(
            sum_dc.reshape(n_expert, cap_rows), "expert", split_axis=0, concat_axis=0, tiled=True
        ),
    )
    grad_tokens = jnp.dot(
        both, back_dx.reshape(width, -1), preferred_element_type=f32
    ).astype(bf16)
    grad_combine = jnp.sum(picks.astype(f32) * back_dc.reshape(width), axis=2)
    return (grad_tokens, grad_combine, grad_w_in[None], grad_b_in[None], grad_w_out[None], grad_b_out[None])


F32, BF16 = jnp.float32, jnp.bfloat16
CORES = 2
LANES = 128


def matmul(left, right, dims):
    return lax.dot_general(left, right, (dims, ((), ())), preferred_element_type=F32)


def split_pair(value, rows):
    high = value.astype(BF16).astype(F32)
    lane = lax.broadcasted_iota(jnp.int32, (rows, LANES), 1)
    return jnp.where(lane < LANES // 2, high, value - high).astype(BF16)


def join_pair(pair):
    return jnp.sum(pair.astype(F32), axis=1, keepdims=True) * (2.0 / LANES)


def fused_kernel(
    n_expert, chips, cap, x_hbm, g_hbm, routes_ref, slots_ref, combine_ref, w_in_hbm, b_in_ref, w_out_hbm, b_out_ref,
    gt_ref, gc_ref, gwi_hbm, gbi_ref, gwo_hbm, gbo_ref,
    w_in_ref, w_out_ref, gwi_ref, gwo_ref, tok, sendbuf, rows, hid, dpre, dout, dx, dxrecv, retsend, retrecv, fsend, frecv, facc,
    tok_s, tok_r, xy_s, xy_r, sib_s, sib_r, dx_s, dx_r, ret_s, ret_r, fin_s, fin_r, loc, part, part_sem,
    mtok, mtok_s, mtok_r,
):
    me_e = lax.axis_index("expert")
    me_z = lax.axis_index("zero")
    chip, core = me_z // CORES, me_z % CORES
    width = n_expert * cap
    toks = tok.shape[1]
    dim = w_in_ref.shape[0]
    units = w_in_ref.shape[1]
    sibling = (me_e, chip * CORES + 1 - core)

    def chunk(index):
        return pl.ds(pl.multiple_of(index * cap, cap), cap)

    def expert_peer(p):
        return lax.rem(me_e + p, n_expert)

    def chip_peer(p):
        return lax.rem(chip + p, chips)

    partner = chip + 1 - 2 * (chip % 2)
    base = chips // 2 * (1 - chip // 2)

    def order(step):
        far = jnp.where(chip < chips // 2, step, chips - 1 - step)
        return jnp.where(step == 0, chip, jnp.where(step == 1, partner, far))

    def remote(src, dst, send, recv, device):
        return pltpu.make_async_remote_copy(
            src_ref=src, dst_ref=dst, send_sem=send, recv_sem=recv, device_id=device,
            device_id_type=pl.DeviceIdType.MESH,
        )

    def tok_copy(src, way):
        to = chip + (1 if way else -1)
        return remote(
            tok.at[src], tok.at[src], tok_s.at[way, src], tok_r.at[src],
            (me_e, to * CORES + core),
        )

    def meta_copy(src, way):
        to = chip + (1 if way else -1)
        return remote(
            mtok.at[src], mtok.at[src], mtok_s.at[way, src], mtok_r.at[src],
            (me_e, to * CORES + core),
        )

    def send_tokens(src, way):
        meta_copy(src, way).start()
        tok_copy(src, way).start()

    def pass_tokens(away):
        @pl.when(chip >= away)
        def _():
            meta_copy(chip - away, 1).wait_recv()
            tok_copy(chip - away, 1).wait_recv()

            @pl.when(chip < chips - 1)
            def _():
                send_tokens(chip - away, 1)

        @pl.when(chip + away < chips)
        def _():
            meta_copy(chip + away, 0).wait_recv()
            tok_copy(chip + away, 0).wait_recv()

            @pl.when(chip > 0)
            def _():
                send_tokens(chip + away, 0)

    def xy_copy(src, peer, frm):
        return remote(
            sendbuf.at[src, chunk(peer)], rows.at[src * CORES + core, chunk(frm)],
            xy_s.at[src, peer], xy_r.at[src, frm], (peer, me_z),
        )

    def sib_copy(src, e, lane):
        return remote(
            rows.at[src * CORES + lane, chunk(e)], rows.at[src * CORES + lane, chunk(e)],
            sib_s.at[src, e], sib_r.at[src, e], sibling,
        )

    def dx_copy(src, lane):
        return remote(
            dx.at[src * CORES + lane], dxrecv.at[src], dx_s.at[src], dx_r.at[src], sibling
        )

    def ret_copy(src, peer, frm):
        return remote(
            retsend.at[src, chunk(peer)], retrecv.at[src, chunk(frm)],
            ret_s.at[src, peer], ret_r.at[src, frm], (peer, me_z),
        )

    def part_copy():
        return remote(
            retsend.at[partner], part, part_sem.at[0], part_sem.at[1],
            (me_e, partner * CORES + core),
        )

    def fin_copy(to, frm):
        return remote(
            fsend.at[to], frecv.at[frm], fin_s.at[to], fin_r.at[frm], (me_e, to * CORES + core)
        )

    def fill_meta():
        slot = slots_ref[...]
        place = jnp.where(slot < cap, routes_ref[...] * cap + slot, -1).astype(F32)
        share = combine_ref[...].astype(F32)
        row = lax.broadcasted_iota(jnp.int32, mtok.shape[1:], 0)
        value = jnp.zeros(mtok.shape[1:], F32)
        for i, line in enumerate((place[0:1], place[1:2], share[0:1], share[1:2])):
            value = jnp.where(row == i, line, value)
        mtok[chip] = value.astype(BF16)

    def picks_of(src):
        meta = mtok[src].astype(F32)
        spots = lax.broadcasted_iota(jnp.int32, (width, toks), 0).astype(F32)
        first = jnp.where(meta[0:1] == spots, 1.0, 0.0)
        second = jnp.where(meta[1:2] == spots, 1.0, 0.0)
        return first, second, meta

    def stage_tokens(src):
        first, second, meta = picks_of(src)
        both = (first + second).astype(BF16)
        step = 512
        for col in range(0, 2 * dim, step):
            out = matmul(both, tok[src, :, col : col + step], ((1,), (0,)))
            sendbuf[src, :, col : col + step] = out.astype(BF16)
        share = jnp.sum(first * meta[2:3] + second * meta[3:4], axis=1, keepdims=True)
        sendbuf[src, :, 2 * dim :] = jnp.broadcast_to(share, (width, LANES)).astype(BF16)
        for p in range(1, n_expert):
            xy_copy(src, expert_peer(p), me_e).start()
        rows[src * CORES + core, chunk(me_e), :] = sendbuf[src, chunk(me_e), :]
        sib_copy(src, me_e, core).start()

    def stage_rows(src):
        for p in range(1, n_expert):
            peer = expert_peer(p)
            xy_copy(src, peer, peer).wait_recv()
            sib_copy(src, peer, core).start()
        for e in range(n_expert):
            sib_copy(src, e, 1 - core).wait_recv()

    def stage_compute(src):
        pair = pl.ds(src * CORES, CORES)
        both = CORES * width
        weight = rows[pair, :, 2 * dim :].reshape(both, LANES).astype(F32)[:, 0:1]
        inner = jnp.zeros((both, 1), F32)
        tile = 256
        for col in range(0, units, tile):
            cols = slice(col, col + tile)
            x = rows[pair, :, :dim].reshape(both, dim)
            pre = matmul(x, w_in_ref[:, cols], ((1,), (0,)))
            pre = pre + b_in_ref[:, cols].astype(F32)
            g = rows[pair, :, dim : 2 * dim].reshape(both, dim)
            back = matmul(g, w_out_ref[cols, :], ((1,), (1,)))
            hidden32, slope = gelu_parts(pre)
            inner = inner + jnp.sum(hidden32 * back, axis=1, keepdims=True)
            hid[pair, :, cols] = hidden32.astype(BF16).reshape(CORES, width, tile)
            dpre[pair, :, cols] = (weight * back * slope).astype(BF16).reshape(CORES, width, tile)
        for col in range(0, dim, 512):
            d = dpre[pair].reshape(both, units)
            out = matmul(d, w_in_ref[col : col + 512, :], ((1,), (1,)))
            dx[pair, :, col : col + 512] = out.astype(BF16).reshape(CORES, width, 512)
        dx[pair, :, dim:] = split_pair(inner, both).reshape(CORES, width, LANES)
        dx_copy(src, 1 - core).start()

    def send_return(src):
        for p in range(1, n_expert):
            ret_copy(src, expert_peer(p), me_e).start()
        retrecv[src, chunk(me_e), :] = retsend[src, chunk(me_e), :]

    def return_own():
        part_copy().wait_recv()
        total = retsend[chip, :, :dim].astype(F32) + part[:, :dim].astype(F32)
        retsend[chip, :, :dim] = total.astype(BF16)
        pair = join_pair(retsend[chip, :, dim:]) + join_pair(part[:, dim:])
        retsend[chip, :, dim:] = split_pair(pair, width)
        send_return(chip)

    def stage_return(src):
        for lane in range(CORES):
            g = src * CORES + lane
            weight = rows[g, :, 2 * dim :].astype(F32)[:, 0:1]
            dout[g] = (weight * rows[g, :, dim : 2 * dim].astype(F32)).astype(BF16)
        g = src * CORES + core
        grads = rows[g, :, dim : 2 * dim].astype(F32)
        bias = jnp.sum(grads * b_out_ref[...].astype(F32), axis=1, keepdims=True)
        bias = bias * jnp.where(src == chip, 1.0, 0.0)
        dx_copy(src, core).wait_recv()
        total = dx[g, :, :dim].astype(F32) + dxrecv[src, :, :dim].astype(F32)
        retsend[src, :, :dim] = total.astype(BF16)
        pair = join_pair(dx[g, :, dim:]) + join_pair(dxrecv[src, :, dim:]) + bias
        retsend[src, :, dim:] = split_pair(pair, width)

        @pl.when(src == partner)
        def _():
            part_copy().start()

        @pl.when((src != partner) & (src != chip))
        def _():
            send_return(src)

    def in_halves(one, two):
        lane = lax.broadcasted_iota(jnp.int32, (toks, LANES), 1)
        return jnp.where(lane < LANES // 2, one, two)

    def stage_combine(src):
        for p in range(1, n_expert):
            peer = expert_peer(p)
            ret_copy(src, peer, peer).wait_recv()
        first, second, _ = picks_of(src)
        both = (first + second).astype(BF16)
        grads = matmul(both, retrecv[src, :, :dim], ((0,), (0,)))
        ext = retrecv[src, :, dim:]
        one = join_pair(matmul(first.astype(BF16), ext, ((0,), (0,))))
        two = join_pair(matmul(second.astype(BF16), ext, ((0,), (0,))))

        @pl.when(src == chip)
        def _():
            facc[:, :dim] = grads
            facc[:, dim:] = in_halves(one, two)

        @pl.when(src != chip)
        def _():
            fsend[src, :, :dim] = grads.astype(BF16)
            high = in_halves(one, two).astype(BF16).astype(F32)
            odd = lax.broadcasted_iota(jnp.int32, (toks, LANES), 1) % 2
            ext = jnp.where(odd == 0, high, in_halves(one, two) - high)
            fsend[src, :, dim:] = ext.astype(BF16)
            fin_copy(src, chip).start()

    barrier = pltpu.get_barrier_semaphore()

    def greet(device):
        pl.semaphore_signal(
            barrier, inc=1, device_id=device, device_id_type=pl.DeviceIdType.MESH
        )

    for p in range(1, n_expert):
        greet((expert_peer(p), me_z))
    for p in range(1, chips):
        greet((me_e, chip_peer(p) * CORES + core))
    greet(sibling)
    loads = [
        pltpu.make_async_copy(src, dst, loc.at[i])
        for i, (src, dst) in enumerate((
            (x_hbm, tok.at[chip, :, :dim]),
            (g_hbm, tok.at[chip, :, dim : 2 * dim]),
            (w_in_hbm, w_in_ref),
            (w_out_hbm, w_out_ref),
        ))
    ]
    for load in loads:
        load.start()
    fill_meta()
    for load in loads[:2]:
        load.wait()
    pl.semaphore_wait(barrier, n_expert + chips - 1)

    @pl.when(chip < chips - 1)
    def _():
        send_tokens(chip, 1)

    @pl.when(chip > 0)
    def _():
        send_tokens(chip, 0)

    @pl.loop(0, chips + 1)
    def _(step):
        @pl.when((step >= 1) & (step < chips))
        def _():
            pass_tokens(step)

        @pl.when(step < chips)
        def _():
            stage_tokens(order(step))

        @pl.when(step == 0)
        def _():
            for load in loads[2:]:
                load.wait()

        @pl.when(step >= 1)
        def _():
            stage_rows(order(step - 1))

        @pl.when(step == chips)
        def _():
            return_own()

        @pl.when(step >= 1)
        def _():
            stage_compute(order(step - 1))
            stage_return(order(step - 1))

        @pl.when(step == chips)
        def _():
            stage_combine(order(step - 2))

    groups = chips * CORES
    all_rows = groups * width

    def weights_in(first, last):
        for col in range(first, last, 256):
            x_all = rows[:, :, col : col + 256].reshape(all_rows, 256)
            d_all = dpre[...].reshape(all_rows, units)
            gwi_ref[col : col + 256, :] = matmul(x_all, d_all, ((0,), (0,))).astype(BF16)

    weights_in(0, dim // 2)
    stage_combine(order(chips - 1))
    stage_combine(chip)
    weights_in(dim // 2, dim)
    store_in = pltpu.make_async_copy(gwi_ref, gwi_hbm, loc.at[5])
    store_in.start()
    o_all = dout[...].reshape(all_rows, dim)
    for col in range(0, units, 256):
        h_all = hid[:, :, col : col + 256].reshape(all_rows, 256)
        gwo_ref[col : col + 256, :] = matmul(h_all, o_all, ((0,), (0,))).astype(BF16)
    store_out = pltpu.make_async_copy(gwo_ref, gwo_hbm, loc.at[6])
    store_out.start()
    ones = jnp.ones((8, all_rows), BF16)
    gbi_ref[...] = matmul(ones, dpre[...].reshape(all_rows, units), ((1,), (0,)))[0:1]
    gbo_ref[...] = matmul(ones, o_all, ((1,), (0,)))[0:1]

    total = facc[:, :dim]
    ext = facc[:, dim:]
    one, two = ext[:, 0:1], ext[:, LANES // 2 : LANES // 2 + 1]
    lane = lax.broadcasted_iota(jnp.int32, (toks, LANES), 1)
    for p in range(chips // 2):
        other = base + p
        fin_copy(other, other).wait_recv()
        total = total + frecv[other, :, :dim].astype(F32)
        ext = frecv[other, :, dim:].astype(F32)
        scale = 4.0 / LANES
        one = one + scale * jnp.sum(
            jnp.where(lane < LANES // 2, ext, 0.0), axis=1, keepdims=True
        )
        two = two + scale * jnp.sum(
            jnp.where(lane < LANES // 2, 0.0, ext), axis=1, keepdims=True
        )
    gt_ref[...] = total.astype(BF16)
    gc_ref[...] = jnp.where(lane == 0, one, two).T[0:TOP]
    store_in.wait()
    store_out.wait()

    part_copy().wait_send()
    for p in range(chips // 2):
        fin_copy(base + p, chip).wait_send()
    for src in range(chips):
        @pl.when((src <= chip) & (chip < chips - 1))
        def _():
            meta_copy(src, 1).wait_send()
            tok_copy(src, 1).wait_send()

        @pl.when((src >= chip) & (chip > 0))
        def _():
            meta_copy(src, 0).wait_send()
            tok_copy(src, 0).wait_send()

        for p in range(1, n_expert):
            xy_copy(src, expert_peer(p), me_e).wait_send()

        @pl.when(src != partner)
        def _():
            for p in range(1, n_expert):
                ret_copy(src, expert_peer(p), me_e).wait_send()

        for e in range(n_expert):
            sib_copy(src, e, core).wait_send()
        dx_copy(src, 1 - core).wait_send()


def hand_over(*refs):
    count = (len(refs) - 1) // 3
    sources, results, middles, sems = refs[:count], refs[count : 2 * count], refs[2 * count : -1], refs[-1]
    loads, stores = [], []
    for src, dst, mid in zip(sources, results, middles):
        pieces = 2 if src.shape[0] >= 64 else 1
        part = src.shape[0] // pieces
        for j in range(pieces):
            at, k = pl.ds(j * part, part), len(loads)
            loads.append(pltpu.make_async_copy(src.at[at], mid.at[at], sems.at[0, k]))
            stores.append(pltpu.make_async_copy(mid.at[at], dst.at[at], sems.at[1, k]))
    for load in loads:
        load.start()
    for load, store in zip(loads, stores):
        load.wait()
        store.start()
    for store in stores:
        store.wait()


def scratch_sizes(n_expert, chips, cap, toks, dim, units):
    width, groups = n_expert * cap, chips * CORES
    return [
        ((dim, units), BF16),
        ((units, dim), BF16),
        ((dim, units), BF16),
        ((units, dim), BF16),
        ((chips, toks, 2 * dim), BF16),
        ((chips, width, 2 * dim + LANES), BF16),
        ((groups, width, 2 * dim + LANES), BF16),
        ((groups, width, units), BF16),
        ((groups, width, units), BF16),
        ((groups, width, dim), BF16),
        ((groups, width, dim + LANES), BF16),
        ((chips, width, dim + LANES), BF16),
        ((chips, width, dim + LANES), BF16),
        ((chips, width, dim + LANES), BF16),
        ((chips, toks, dim + LANES), BF16),
        ((chips, toks, dim + LANES), BF16),
        ((toks, dim + LANES), F32),
    ]


def on_device(tokens, grads_out, routes, slots, combine, w_in, b_in, w_out, b_out):
    n_expert = lax.axis_size("expert")
    n_zero = lax.axis_size("zero")
    toks, dim = tokens.shape
    units = w_in.shape[2]
    cap = TOP * toks // n_expert
    chips = n_zero // CORES
    sizes = scratch_sizes(n_expert, chips, cap, toks, dim, units)
    held = sum(functools.reduce(lambda a, b: a * b, s) * jnp.dtype(t).itemsize for s, t in sizes)
    if held > (46 << 20) or n_expert * cap > 256 or n_zero % CORES or chips != 4 or toks != LANES:
        return plain_device(
            tokens, grads_out, routes, slots, combine, w_in, b_in, w_out, b_out
        )
    vmem = pl.BlockSpec(memory_space=pltpu.VMEM)
    hbm = pl.BlockSpec(memory_space=pl.ANY)
    sem = pltpu.SemaphoreType.DMA
    outs = pl.pallas_call(
        functools.partial(fused_kernel, n_expert, chips, cap),
        out_shape=(
            jax.ShapeDtypeStruct((toks, dim), BF16),
            jax.ShapeDtypeStruct((TOP, toks), F32),
            jax.ShapeDtypeStruct((dim, units), BF16),
            jax.ShapeDtypeStruct((1, units), F32),
            jax.ShapeDtypeStruct((units, dim), BF16),
            jax.ShapeDtypeStruct((1, dim), F32),
        ),
        in_specs=[hbm, hbm, vmem, vmem, vmem, hbm, vmem, hbm, vmem],
        out_specs=(vmem, vmem, hbm, vmem, hbm, vmem),
        scratch_shapes=[pltpu.VMEM(s, t) for s, t in sizes]
        + [
            sem((2, chips)), sem((chips,)),
            sem((chips, n_expert)), sem((chips, n_expert)),
            sem((chips, n_expert)), sem((chips, n_expert)),
            sem((chips,)), sem((chips,)),
            sem((chips, n_expert)), sem((chips, n_expert)),
            sem((chips,)), sem((chips,)),
            sem((7,)),
            pltpu.VMEM((n_expert * cap, dim + LANES), BF16),
            sem((2,)),
            pltpu.VMEM((chips, 16, toks), BF16),
            sem((2, chips)),
            sem((chips,)),
        ],
        compiler_params=pltpu.CompilerParams(
            collective_id=0, has_side_effects=True, vmem_limit_bytes=60 << 20
        ),
        name="routed_expert_backward",
    )(tokens, grads_out, routes.T, slots.T, combine.T, w_in[0], b_in, w_out[0], b_out)
    outs = pl.pallas_call(
        hand_over,
        out_shape=tuple(jax.ShapeDtypeStruct(a.shape, a.dtype) for a in outs),
        in_specs=[hbm] * len(outs),
        out_specs=(hbm,) * len(outs),
        scratch_shapes=[pltpu.VMEM(a.shape, a.dtype) for a in outs] + [sem((2, 12))],
        compiler_params=pltpu.CompilerParams(vmem_limit_bytes=60 << 20),
        name="hand_over",
    )(*outs)
    gt, gc, gwi, gbi, gwo, gbo = outs
    return (gt, gc.T, gwi[None], gbi, gwo[None], gbo)


def solution(mesh):
    in_specs = (
        P(("expert", "zero"), None),
        P(("expert", "zero"), None),
        P(("expert", "zero"), None),
        P(("expert", "zero"), None),
        P(("expert", "zero"), None),
        P("expert", None, "zero"),
        P("expert", "zero"),
        P("expert", "zero", None),
        P("expert", None),
    )
    out_specs = (
        P(("expert", "zero"), None),
        P(("expert", "zero"), None),
        P("expert", None, "zero"),
        P("expert", "zero"),
        P("expert", "zero", None),
        P("expert", None),
    )
    return jax.shard_map(
        on_device, mesh=mesh, in_specs=in_specs, out_specs=out_specs, check_vma=False
    )
```

```python
import functools

import jax
import jax.numpy as jnp
from jax import lax
from jax.experimental import pallas as pl
from jax.experimental.pallas import tpu as pltpu
from jax.sharding import PartitionSpec as P

TOP = 2


def gelu_parts(pre):
    cdf = 0.5 * (1.0 + lax.erf(pre * 0.7071067811865476))
    dens = jnp.exp(-0.5 * pre * pre) * 0.3989422804014327
    return (pre * cdf, cdf + pre * dens)


def plain_device(tokens, grads_out, routes, slots, combine, w_in, b_in, w_out, b_out):
    f32, bf16 = jnp.float32, jnp.bfloat16
    n_expert = lax.axis_size("expert")
    n_zero = lax.axis_size("zero")
    tok_rows, dim = tokens.shape
    cap_rows = TOP * tok_rows // n_expert
    width = n_expert * cap_rows
    spots = jnp.arange(width, dtype=jnp.int32)
    places = jnp.where(slots < cap_rows, routes * cap_rows + slots, -1)
    picks = (places[:, :, None] == spots[None, None, :]).astype(bf16)
    both = picks[:, 0] + picks[:, 1]
    pair = jnp.concatenate([tokens, grads_out], axis=1)
    send = jnp.einsum("tp,td->pd", both, pair, preferred_element_type=f32).astype(bf16)
    send_c = jnp.einsum("tkp,tk->p", picks, combine, preferred_element_type=f32).astype(bf16)
    send = jnp.concatenate([send, jnp.broadcast_to(send_c[:, None], (width, 128))], axis=1)
    got = lax.all_to_all(
        send.reshape(n_expert, cap_rows, -1), "expert", split_axis=0, concat_axis=0, tiled=True
    ).reshape(width, -1)
    rows = lax.all_gather(got, "zero", axis=0, tiled=True)
    rows_x = rows[:, :dim]
    rows_g = rows[:, dim : 2 * dim]
    weight = rows[:, 2 * dim : 2 * dim + 1].astype(f32)
    pre = jnp.dot(rows_x, w_in[0], preferred_element_type=f32) + b_in.astype(f32)
    hidden32, slope = gelu_parts(pre)
    back = jnp.einsum("rd,fd->rf", rows_g, w_out[0], preferred_element_type=f32)
    inner = jnp.sum(hidden32 * back, axis=1)
    hidden = hidden32.astype(bf16)
    dpre = (weight * back * slope).astype(bf16)
    dout = (weight * rows_g.astype(f32)).astype(bf16)
    slot_dx = jnp.einsum("rf,df->rd", dpre, w_in[0], preferred_element_type=f32).astype(bf16)
    part_dx = lax.all_to_all(
        slot_dx.reshape(n_zero, width, dim), "zero", split_axis=0, concat_axis=0, tiled=True
    )
    sum_dx = jnp.sum(part_dx.astype(f32), axis=0).astype(bf16)
    part_dc = lax.all_to_all(
        inner.reshape(n_zero, width), "zero", split_axis=0, concat_axis=0, tiled=True
    )
    bias_dc = jnp.sum(got[:, dim : 2 * dim].astype(f32) * b_out.astype(f32), axis=1)
    sum_dc = jnp.sum(part_dc, axis=0) + bias_dc
    grad_w_in = jnp.einsum("ra,rb->ab", rows_x, dpre, preferred_element_type=f32).astype(bf16)
    grad_w_out = jnp.einsum("ra,rb->ab", hidden, dout, preferred_element_type=f32).astype(bf16)
    grad_b_in = jnp.sum(dpre.astype(f32), axis=0)
    grad_b_out = jnp.sum(dout.astype(f32), axis=0)
    back_dx, back_dc = (
        lax.all_to_all(
            sum_dx.reshape(n_expert, cap_rows, -1), "expert", split_axis=0, concat_axis=0, tiled=True
        ),
        lax.all_to_all(
            sum_dc.reshape(n_expert, cap_rows), "expert", split_axis=0, concat_axis=0, tiled=True
        ),
    )
    grad_tokens = jnp.dot(
        both, back_dx.reshape(width, -1), preferred_element_type=f32
    ).astype(bf16)
    grad_combine = jnp.sum(picks.astype(f32) * back_dc.reshape(width), axis=2)
    return (grad_tokens, grad_combine, grad_w_in[None], grad_b_in[None], grad_w_out[None], grad_b_out[None])


F32, BF16 = jnp.float32, jnp.bfloat16
CORES = 2
LANES = 128


def matmul(left, right, dims):
    return lax.dot_general(left, right, (dims, ((), ())), preferred_element_type=F32)


def split_pair(value, rows):
    high = value.astype(BF16).astype(F32)
    lane = lax.broadcasted_iota(jnp.int32, (rows, LANES), 1)
    return jnp.where(lane < LANES // 2, high, value - high).astype(BF16)


def join_pair(pair):
    return jnp.sum(pair.astype(F32), axis=1, keepdims=True) * (2.0 / LANES)


def fused_kernel(
    n_expert, chips, cap, x_hbm, g_hbm, routes_ref, slots_ref, combine_ref, w_in_hbm, b_in_ref, w_out_hbm, b_out_ref,
    gt_ref, gc_ref, gwi_hbm, gbi_ref, gwo_hbm, gbo_ref,
    w_in_ref, w_out_ref, gwi_ref, gwo_ref, tok, sendbuf, rows, hid, dpre, dout, dx, dxrecv, retsend, retrecv, fsend, frecv, facc,
    tok_s, tok_r, xy_s, xy_r, sib_s, sib_r, dx_s, dx_r, ret_s, ret_r, fin_s, fin_r, loc, part, part_sem,
    mtok, mtok_s, mtok_r,
):
    me_e = lax.axis_index("expert")
    me_z = lax.axis_index("zero")
    chip, core = me_z // CORES, me_z % CORES
    width = n_expert * cap
    toks = tok.shape[1]
    dim = w_in_ref.shape[0]
    units = w_in_ref.shape[1]
    sibling = (me_e, chip * CORES + 1 - core)

    def chunk(index):
        return pl.ds(pl.multiple_of(index * cap, cap), cap)

    def expert_peer(p):
        return lax.rem(me_e + p, n_expert)

    def chip_peer(p):
        return lax.rem(chip + p, chips)

    partner = chip + 1 - 2 * (chip % 2)
    base = chips // 2 * (1 - chip // 2)

    def order(step):
        far = jnp.where(chip < chips // 2, step, chips - 1 - step)
        return jnp.where(step == 0, chip, jnp.where(step == 1, partner, far))

    def remote(src, dst, send, recv, device):
        return pltpu.make_async_remote_copy(
            src_ref=src, dst_ref=dst, send_sem=send, recv_sem=recv, device_id=device,
            device_id_type=pl.DeviceIdType.MESH,
        )

    def tok_copy(src, way):
        to = chip + (1 if way else -1)
        return remote(
            tok.at[src], tok.at[src], tok_s.at[way, src], tok_r.at[src],
            (me_e, to * CORES + core),
        )

    def meta_copy(src, way):
        to = chip + (1 if way else -1)
        return remote(
            mtok.at[src], mtok.at[src], mtok_s.at[way, src], mtok_r.at[src],
            (me_e, to * CORES + core),
        )

    def send_tokens(src, way):
        meta_copy(src, way).start()
        tok_copy(src, way).start()

    def pass_tokens(away):
        @pl.when(chip >= away)
        def _():
            meta_copy(chip - away, 1).wait_recv()
            tok_copy(chip - away, 1).wait_recv()

            @pl.when(chip < chips - 1)
            def _():
                send_tokens(chip - away, 1)

        @pl.when(chip + away < chips)
        def _():
            meta_copy(chip + away, 0).wait_recv()
            tok_copy(chip + away, 0).wait_recv()

            @pl.when(chip > 0)
            def _():
                send_tokens(chip + away, 0)

    def xy_copy(src, peer, frm):
        return remote(
            sendbuf.at[src, chunk(peer)], rows.at[src * CORES + core, chunk(frm)],
            xy_s.at[src, peer], xy_r.at[src, frm], (peer, me_z),
        )

    def sib_copy(src, e, lane):
        return remote(
            rows.at[src * CORES + lane, chunk(e)], rows.at[src * CORES + lane, chunk(e)],
            sib_s.at[src, e], sib_r.at[src, e], sibling,
        )

    def dx_copy(src, lane):
        return remote(
            dx.at[src * CORES + lane], dxrecv.at[src], dx_s.at[src], dx_r.at[src], sibling
        )

    def ret_copy(src, peer, frm):
        return remote(
            retsend.at[src, chunk(peer)], retrecv.at[src, chunk(frm)],
            ret_s.at[src, peer], ret_r.at[src, frm], (peer, me_z),
        )

    def part_copy():
        return remote(
            retsend.at[partner], part, part_sem.at[0], part_sem.at[1],
            (me_e, partner * CORES + core),
        )

    def fin_copy(to, frm):
        return remote(
            fsend.at[to], frecv.at[frm], fin_s.at[to], fin_r.at[frm], (me_e, to * CORES + core)
        )

    def fill_meta():
        slot = slots_ref[...]
        place = jnp.where(slot < cap, routes_ref[...] * cap + slot, -1).astype(F32)
        share = combine_ref[...].astype(F32)
        row = lax.broadcasted_iota(jnp.int32, mtok.shape[1:], 0)
        value = jnp.zeros(mtok.shape[1:], F32)
        for i, line in enumerate((place[0:1], place[1:2], share[0:1], share[1:2])):
            value = jnp.where(row == i, line, value)
        mtok[chip] = value.astype(BF16)

    def picks_of(src):
        meta = mtok[src].astype(F32)
        spots = lax.broadcasted_iota(jnp.int32, (width, toks), 0).astype(F32)
        first = jnp.where(meta[0:1] == spots, 1.0, 0.0)
        second = jnp.where(meta[1:2] == spots, 1.0, 0.0)
        return first, second, meta

    def stage_tokens(src):
        first, second, meta = picks_of(src)
        both = (first + second).astype(BF16)
        step = 512
        for col in range(0, 2 * dim, step):
            out = matmul(both, tok[src, :, col : col + step], ((1,), (0,)))
            sendbuf[src, :, col : col + step] = out.astype(BF16)
        share = jnp.sum(first * meta[2:3] + second * meta[3:4], axis=1, keepdims=True)
        sendbuf[src, :, 2 * dim :] = jnp.broadcast_to(share, (width, LANES)).astype(BF16)
        for p in range(1, n_expert):
            xy_copy(src, expert_peer(p), me_e).start()
        rows[src * CORES + core, chunk(me_e), :] = sendbuf[src, chunk(me_e), :]
        sib_copy(src, me_e, core).start()

    def stage_rows(src):
        for p in range(1, n_expert):
            peer = expert_peer(p)
            xy_copy(src, peer, peer).wait_recv()
            sib_copy(src, peer, core).start()
        for e in range(n_expert):
            sib_copy(src, e, 1 - core).wait_recv()

    def stage_compute(src):
        pair = pl.ds(src * CORES, CORES)
        both = CORES * width
        weight = rows[pair, :, 2 * dim :].reshape(both, LANES).astype(F32)[:, 0:1]
        inner = jnp.zeros((both, 1), F32)
        tile = 256
        for col in range(0, units, tile):
            cols = slice(col, col + tile)
            x = rows[pair, :, :dim].reshape(both, dim)
            pre = matmul(x, w_in_ref[:, cols], ((1,), (0,)))
            pre = pre + b_in_ref[:, cols].astype(F32)
            g = rows[pair, :, dim : 2 * dim].reshape(both, dim)
            back = matmul(g, w_out_ref[cols, :], ((1,), (1,)))
            hidden32, slope = gelu_parts(pre)
            inner = inner + jnp.sum(hidden32 * back, axis=1, keepdims=True)
            hid[pair, :, cols] = hidden32.astype(BF16).reshape(CORES, width, tile)
            dpre[pair, :, cols] = (weight * back * slope).astype(BF16).reshape(CORES, width, tile)
        for col in range(0, dim, 512):
            d = dpre[pair].reshape(both, units)
            out = matmul(d, w_in_ref[col : col + 512, :], ((1,), (1,)))
            dx[pair, :, col : col + 512] = out.astype(BF16).reshape(CORES, width, 512)
        dx[pair, :, dim:] = split_pair(inner, both).reshape(CORES, width, LANES)
        dx_copy(src, 1 - core).start()

    def send_return(src):
        for p in range(1, n_expert):
            ret_copy(src, expert_peer(p), me_e).start()
        retrecv[src, chunk(me_e), :] = retsend[src, chunk(me_e), :]

    def add_part():
        grads = rows[chip * CORES + core, :, dim : 2 * dim].astype(F32)
        bias = jnp.sum(grads * b_out_ref[...].astype(F32), axis=1, keepdims=True)
        part_copy().wait_recv()
        total = retsend[chip, :, :dim].astype(F32) + part[:, :dim].astype(F32)
        retsend[chip, :, :dim] = total.astype(BF16)
        pair = join_pair(retsend[chip, :, dim:]) + join_pair(part[:, dim:]) + bias
        retsend[chip, :, dim:] = split_pair(pair, width)

    def stage_return(src):
        for lane in range(CORES):
            g = src * CORES + lane
            weight = rows[g, :, 2 * dim :].astype(F32)[:, 0:1]
            dout[g] = (weight * rows[g, :, dim : 2 * dim].astype(F32)).astype(BF16)
        g = src * CORES + core
        dx_copy(src, core).wait_recv()
        total = dx[g, :, :dim].astype(F32) + dxrecv[src, :, :dim].astype(F32)
        retsend[src, :, :dim] = total.astype(BF16)
        pair = join_pair(dx[g, :, dim:]) + join_pair(dxrecv[src, :, dim:])
        retsend[src, :, dim:] = split_pair(pair, width)

        @pl.when(src == partner)
        def _():
            part_copy().start()

        @pl.when((src != partner) & (src != chip))
        def _():
            send_return(src)

    def in_halves(one, two):
        lane = lax.broadcasted_iota(jnp.int32, (toks, LANES), 1)
        return jnp.where(lane < LANES // 2, one, two)

    def stage_combine(src):
        for p in range(1, n_expert):
            peer = expert_peer(p)
            ret_copy(src, peer, peer).wait_recv()
        first, second, _ = picks_of(src)
        both = (first + second).astype(BF16)
        grads = matmul(both, retrecv[src, :, :dim], ((0,), (0,)))
        ext = retrecv[src, :, dim:]
        one = join_pair(matmul(first.astype(BF16), ext, ((0,), (0,))))
        two = join_pair(matmul(second.astype(BF16), ext, ((0,), (0,))))

        @pl.when(src == chip)
        def _():
            facc[:, :dim] = grads
            facc[:, dim:] = in_halves(one, two)

        @pl.when(src != chip)
        def _():
            fsend[src, :, :dim] = grads.astype(BF16)
            high = in_halves(one, two).astype(BF16).astype(F32)
            odd = lax.broadcasted_iota(jnp.int32, (toks, LANES), 1) % 2
            ext = jnp.where(odd == 0, high, in_halves(one, two) - high)
            fsend[src, :, dim:] = ext.astype(BF16)
            fin_copy(src, chip).start()

    barrier = pltpu.get_barrier_semaphore()

    def greet(device):
        pl.semaphore_signal(
            barrier, inc=1, device_id=device, device_id_type=pl.DeviceIdType.MESH
        )

    for p in range(1, n_expert):
        greet((expert_peer(p), me_z))
    for p in range(1, chips):
        greet((me_e, chip_peer(p) * CORES + core))
    greet(sibling)
    loads = [
        pltpu.make_async_copy(src, dst, loc.at[i])
        for i, (src, dst) in enumerate((
            (x_hbm, tok.at[chip, :, :dim]),
            (g_hbm, tok.at[chip, :, dim : 2 * dim]),
            (w_in_hbm, w_in_ref),
            (w_out_hbm, w_out_ref),
        ))
    ]
    for load in loads:
        load.start()
    fill_meta()
    for load in loads[:2]:
        load.wait()
    pl.semaphore_wait(barrier, n_expert + chips - 1)

    @pl.when(chip < chips - 1)
    def _():
        send_tokens(chip, 1)

    @pl.when(chip > 0)
    def _():
        send_tokens(chip, 0)

    @pl.loop(0, chips + 1)
    def _(step):
        @pl.when((step >= 1) & (step < chips))
        def _():
            pass_tokens(step)

        @pl.when(step < chips)
        def _():
            stage_tokens(order(step))

        @pl.when(step == 0)
        def _():
            for load in loads[2:]:
                load.wait()

        @pl.when(step == chips)
        def _():
            add_part()

        @pl.when(step >= 1)
        def _():
            stage_rows(order(step - 1))

        @pl.when(step == chips)
        def _():
            send_return(chip)

        @pl.when(step >= 1)
        def _():
            stage_compute(order(step - 1))
            stage_return(order(step - 1))

        @pl.when(step == chips)
        def _():
            stage_combine(order(step - 2))

    groups = chips * CORES
    all_rows = groups * width

    def weights_in(first, last):
        for col in range(first, last, 256):
            x_all = rows[:, :, col : col + 256].reshape(all_rows, 256)
            d_all = dpre[...].reshape(all_rows, units)
            gwi_ref[col : col + 256, :] = matmul(x_all, d_all, ((0,), (0,))).astype(BF16)

    weights_in(0, dim // 2)
    stage_combine(order(chips - 1))
    stage_combine(chip)
    weights_in(dim // 2, dim)
    store_in = pltpu.make_async_copy(gwi_ref, gwi_hbm, loc.at[5])
    store_in.start()
    o_all = dout[...].reshape(all_rows, dim)
    for col in range(0, units, 256):
        h_all = hid[:, :, col : col + 256].reshape(all_rows, 256)
        gwo_ref[col : col + 256, :] = matmul(h_all, o_all, ((0,), (0,))).astype(BF16)
    store_out = pltpu.make_async_copy(gwo_ref, gwo_hbm, loc.at[6])
    store_out.start()
    ones = jnp.ones((8, all_rows), BF16)
    gbi_ref[...] = matmul(ones, dpre[...].reshape(all_rows, units), ((1,), (0,)))[0:1]
    gbo_ref[...] = matmul(ones, o_all, ((1,), (0,)))[0:1]

    total = facc[:, :dim]
    ext = facc[:, dim:]
    one, two = ext[:, 0:1], ext[:, LANES // 2 : LANES // 2 + 1]
    lane = lax.broadcasted_iota(jnp.int32, (toks, LANES), 1)
    for p in range(chips // 2):
        other = base + p
        fin_copy(other, other).wait_recv()
        total = total + frecv[other, :, :dim].astype(F32)
        ext = frecv[other, :, dim:].astype(F32)
        scale = 4.0 / LANES
        one = one + scale * jnp.sum(
            jnp.where(lane < LANES // 2, ext, 0.0), axis=1, keepdims=True
        )
        two = two + scale * jnp.sum(
            jnp.where(lane < LANES // 2, 0.0, ext), axis=1, keepdims=True
        )
    gt_ref[...] = total.astype(BF16)
    gc_ref[...] = jnp.where(lane == 0, one, two).T[0:TOP]
    store_in.wait()
    store_out.wait()

    part_copy().wait_send()
    for p in range(chips // 2):
        fin_copy(base + p, chip).wait_send()
    for src in range(chips):
        @pl.when((src <= chip) & (chip < chips - 1))
        def _():
            meta_copy(src, 1).wait_send()
            tok_copy(src, 1).wait_send()

        @pl.when((src >= chip) & (chip > 0))
        def _():
            meta_copy(src, 0).wait_send()
            tok_copy(src, 0).wait_send()

        for p in range(1, n_expert):
            xy_copy(src, expert_peer(p), me_e).wait_send()

        @pl.when(src != partner)
        def _():
            for p in range(1, n_expert):
                ret_copy(src, expert_peer(p), me_e).wait_send()

        for e in range(n_expert):
            sib_copy(src, e, core).wait_send()
        dx_copy(src, 1 - core).wait_send()


def hand_over(*refs):
    count = (len(refs) - 1) // 3
    sources, results, middles, sems = refs[:count], refs[count : 2 * count], refs[2 * count : -1], refs[-1]
    loads, stores = [], []
    for src, dst, mid in zip(sources, results, middles):
        pieces = 2 if src.shape[0] >= 64 else 1
        part = src.shape[0] // pieces
        for j in range(pieces):
            at, k = pl.ds(j * part, part), len(loads)
            loads.append(pltpu.make_async_copy(src.at[at], mid.at[at], sems.at[0, k]))
            stores.append(pltpu.make_async_copy(mid.at[at], dst.at[at], sems.at[1, k]))
    for load in loads:
        load.start()
    for load, store in zip(loads, stores):
        load.wait()
        store.start()
    for store in stores:
        store.wait()


def scratch_sizes(n_expert, chips, cap, toks, dim, units):
    width, groups = n_expert * cap, chips * CORES
    return [
        ((dim, units), BF16),
        ((units, dim), BF16),
        ((dim, units), BF16),
        ((units, dim), BF16),
        ((chips, toks, 2 * dim), BF16),
        ((chips, width, 2 * dim + LANES), BF16),
        ((groups, width, 2 * dim + LANES), BF16),
        ((groups, width, units), BF16),
        ((groups, width, units), BF16),
        ((groups, width, dim), BF16),
        ((groups, width, dim + LANES), BF16),
        ((chips, width, dim + LANES), BF16),
        ((chips, width, dim + LANES), BF16),
        ((chips, width, dim + LANES), BF16),
        ((chips, toks, dim + LANES), BF16),
        ((chips, toks, dim + LANES), BF16),
        ((toks, dim + LANES), F32),
    ]


def on_device(tokens, grads_out, routes, slots, combine, w_in, b_in, w_out, b_out):
    n_expert = lax.axis_size("expert")
    n_zero = lax.axis_size("zero")
    toks, dim = tokens.shape
    units = w_in.shape[2]
    cap = TOP * toks // n_expert
    chips = n_zero // CORES
    sizes = scratch_sizes(n_expert, chips, cap, toks, dim, units)
    held = sum(functools.reduce(lambda a, b: a * b, s) * jnp.dtype(t).itemsize for s, t in sizes)
    if held > (46 << 20) or n_expert * cap > 256 or n_zero % CORES or chips != 4 or toks != LANES:
        return plain_device(
            tokens, grads_out, routes, slots, combine, w_in, b_in, w_out, b_out
        )
    vmem = pl.BlockSpec(memory_space=pltpu.VMEM)
    hbm = pl.BlockSpec(memory_space=pl.ANY)
    sem = pltpu.SemaphoreType.DMA
    outs = pl.pallas_call(
        functools.partial(fused_kernel, n_expert, chips, cap),
        out_shape=(
            jax.ShapeDtypeStruct((toks, dim), BF16),
            jax.ShapeDtypeStruct((TOP, toks), F32),
            jax.ShapeDtypeStruct((dim, units), BF16),
            jax.ShapeDtypeStruct((1, units), F32),
            jax.ShapeDtypeStruct((units, dim), BF16),
            jax.ShapeDtypeStruct((1, dim), F32),
        ),
        in_specs=[hbm, hbm, vmem, vmem, vmem, hbm, vmem, hbm, vmem],
        out_specs=(vmem, vmem, hbm, vmem, hbm, vmem),
        scratch_shapes=[pltpu.VMEM(s, t) for s, t in sizes]
        + [
            sem((2, chips)), sem((chips,)),
            sem((chips, n_expert)), sem((chips, n_expert)),
            sem((chips, n_expert)), sem((chips, n_expert)),
            sem((chips,)), sem((chips,)),
            sem((chips, n_expert)), sem((chips, n_expert)),
            sem((chips,)), sem((chips,)),
            sem((7,)),
            pltpu.VMEM((n_expert * cap, dim + LANES), BF16),
            sem((2,)),
            pltpu.VMEM((chips, 16, toks), BF16),
            sem((2, chips)),
            sem((chips,)),
        ],
        compiler_params=pltpu.CompilerParams(
            collective_id=0, has_side_effects=True, vmem_limit_bytes=60 << 20
        ),
        name="routed_expert_backward",
    )(tokens, grads_out, routes.T, slots.T, combine.T, w_in[0], b_in, w_out[0], b_out)
    outs = pl.pallas_call(
        hand_over,
        out_shape=tuple(jax.ShapeDtypeStruct(a.shape, a.dtype) for a in outs),
        in_specs=[hbm] * len(outs),
        out_specs=(hbm,) * len(outs),
        scratch_shapes=[pltpu.VMEM(a.shape, a.dtype) for a in outs] + [sem((2, 12))],
        compiler_params=pltpu.CompilerParams(vmem_limit_bytes=60 << 20),
        name="hand_over",
    )(*outs)
    gt, gc, gwi, gbi, gwo, gbo = outs
    return (gt, gc.T, gwi[None], gbi, gwo[None], gbo)


def solution(mesh):
    in_specs = (
        P(("expert", "zero"), None),
        P(("expert", "zero"), None),
        P(("expert", "zero"), None),
        P(("expert", "zero"), None),
        P(("expert", "zero"), None),
        P("expert", None, "zero"),
        P("expert", "zero"),
        P("expert", "zero", None),
        P("expert", None),
    )
    out_specs = (
        P(("expert", "zero"), None),
        P(("expert", "zero"), None),
        P("expert", None, "zero"),
        P("expert", "zero"),
        P("expert", "zero", None),
        P("expert", None),
    )
    return jax.shard_map(
        on_device, mesh=mesh, in_specs=in_specs, out_specs=out_specs, check_vma=False
    )
```
